32 devices in a mesh: wide: 8 (over z, x), narrow: 4 (over y, core).
Axes of the slice: x: 2, y: 2, z: 4, core: 2. Of those that a mesh axis runs over, the one named last changes fastest.
Arguments:
- inputs: bfloat16 [2, 32, 512, 768], P(None, ('wide', 'narrow')), may hold values from -6 to 6
- cotangent: bfloat16 [2, 32, 512, 768], P(None, ('wide', 'narrow')), may hold values from -6 to 6
- doc_ids: int32 [2, 32, 512], P(None, ('wide', 'narrow')), may hold values from 0 to 7, never falling along the last dimension, each value on 1 to 128 neighbouring positions
- attention_weights: float32 [4, 768, 768], P(None, ('wide', 'narrow'))
- attention_momentum: float32 [4, 768, 768], P(None, ('wide', 'narrow')), may hold values from -1024 to 1024
- attention_average: float32 [4, 768, 768], P(None, ('wide', 'narrow'))
- feedforward_weights: float32 [2, 768, 3072], P(None, ('wide', 'narrow'))
- feedforward_momentum: float32 [2, 768, 3072], P(None, ('wide', 'narrow')), may hold values from -1024 to 1024
- feedforward_average: float32 [2, 768, 3072], P(None, ('wide', 'narrow'))
- vector_weights: float32 [12, 768], P(None, ('wide', 'narrow'))
- vector_momentum: float32 [12, 768], P(None, ('wide', 'narrow')), may hold values from -1024 to 1024
- vector_average: float32 [12, 768], P(None, ('wide', 'narrow'))
Outputs:
- layer_out: bfloat16 [2, 32, 512, 768], P(None, ('wide', 'narrow'))
- input_grad: bfloat16 [2, 32, 512, 768], P(None, ('wide', 'narrow'))
- attention_next: float32 [4, 768, 768], P(None, ('wide', 'narrow'))
- attention_buffer: float32 [4, 768, 768], P(None, ('wide', 'narrow'))
- attention_trailing: float32 [4, 768, 768], P(None, ('wide', 'narrow'))
- attention_copy: bfloat16 [4, 768, 768], P(None, ('wide', 'narrow'))
- feedforward_next: float32 [2, 768, 3072], P(None, ('wide', 'narrow'))
- feedforward_buffer: float32 [2, 768, 3072], P(None, ('wide', 'narrow'))
- feedforward_trailing: float32 [2, 768, 3072], P(None, ('wide', 'narrow'))
- feedforward_copy: bfloat16 [2, 768, 3072], P(None, ('wide', 'narrow'))
- vector_next: float32 [12, 768], P(None, ('wide', 'narrow'))
- vector_buffer: float32 [12, 768], P(None, ('wide', 'narrow'))
- vector_trailing: float32 [12, 768], P(None, ('wide', 'narrow'))
- vector_copy: bfloat16 [12, 768], P(None, ('wide', 'narrow'))
The draws below stay inside these ranges and needn't reach their ends.
Inputs may be any that keep to these rules, and one draw needn't show every extreme that they name: `doc_ids`: in each packed row the example number starts at 0, never falls, rises by at most one from a token to the next and ends at 7; an example has at most 128 tokens.
All inputs are finite; a program needn't handle non-finite values.
Results may differ from the reference program's by a relative error of at most 0.012.
The reference program's roundings to bfloat16 on the way count: a program that leaves them out, or rounds other values in their place, can miss the bound.
Values may be sent and summed in bfloat16 or wider, within the bound.
No kernel may reach another device: no remote copies, remote signals or barrier semaphores. Data moves between devices by JAX's collectives and lax.ppermute only.
A program may use at most 512 MiB of HBM per device.

```python
import math
from functools import partial
import jax
import jax.numpy as jnp
import numpy as np
from jax import lax

D = 768
HEADS = 12
HEAD_DIM = 64
FF = 3072
MICRO = 2
ROW_LEN = 512
ROWS = 32
TOKENS = 32768
NV = 12
DOCS = 8
DOC_MOST = 128


def scaled_normal(key, array_shape, scales):
    values = jax.random.normal(key, array_shape, jnp.float32)
    factor = jnp.asarray(scales, jnp.float32).reshape((-1,) + (1,) * (len(array_shape) - 1))
    return values * factor


def attention_scales():
    return [D ** (-0.5), D ** (-0.5), D ** (-0.5), (8.0 / D) ** 0.5]


def feedforward_scales():
    return [D ** (-0.5), FF ** (-0.5)]


def vector_table(key):
    key_one, key_two = jax.random.split(key)
    bias_values = 0.3 * jax.random.normal(key_one, (NV, D), jnp.float32)
    gain_values = jax.random.uniform(key_two, (NV, D), jnp.float32, 0.6, 1.6)
    row_index = jnp.arange(NV)[:, None]
    blocks = FF // D
    is_gain = (row_index == blocks + 4) | (row_index == blocks + 6)
    return jnp.where(is_gain, gain_values, bias_values)


def draw_attention_weights(key, part):
    key = jax.random.fold_in(key, 11)
    return scaled_normal(key, (4, D, D), attention_scales())


def draw_attention_average(key, part):
    key = jax.random.fold_in(key, 12)
    return scaled_normal(key, (4, D, D), attention_scales())


def draw_feedforward_weights(key, part):
    key = jax.random.fold_in(key, 13)
    return scaled_normal(key, (2, D, FF), feedforward_scales())


def draw_feedforward_average(key, part):
    key = jax.random.fold_in(key, 14)
    return scaled_normal(key, (2, D, FF), feedforward_scales())


def draw_vector_weights(key, part):
    key = jax.random.fold_in(key, 15)
    return vector_table(key)


def draw_vector_average(key, part):
    key = jax.random.fold_in(key, 16)
    return vector_table(key)


def with_spikes(entries, stream_key, source, target, shards_of, factor):
    def block_of(axis_at):
        return (jnp.arange(entries.shape[axis_at]) // (entries.shape[axis_at] // shards_of)).reshape((-1,) + (1,) * (entries.ndim - 1 - axis_at))

    one_side = jax.random.permutation(stream_key, shards_of)[block_of(target)]
    far = (block_of(target) + shards_of // 2) % shards_of
    return jnp.where((block_of(source) == one_side) | (block_of(source) == far), factor * entries, entries)


def block_levels(own_key, shape, pieces, least, top_value):
    def one(axis_at, parts):
        heights = jax.random.uniform(jax.random.fold_in(jax.random.fold_in(own_key, 6), axis_at), (parts,), jnp.float32, least / len(pieces), top_value / len(pieces))
        return jnp.repeat(jnp.exp(heights), shape[axis_at] // parts).reshape((-1,) + (1,) * (len(shape) - axis_at - 1))

    level = one(*pieces[0])
    for cut in pieces[1:]:
        level = level * one(*cut)
    return level


def split_up(count, total, bound, slope):
    loads = [(1 << 20) // math.isqrt(grade ** slope) + 1 for grade in range(2, count + 1)]
    rest, given = total - bound - (count - 1), [1] * (count - 1)
    while rest > 0:
        free = [i for i in range(count - 1) if given[i] < bound]
        whole, budget = sum([loads[i] for i in free]), rest
        for i in free:
            addition = min(bound - given[i], max(1, budget * loads[i] // whole), rest)
            given[i] = given[i] + addition
            rest = rest - addition
    return np.array([bound] + given)


def uneven_parts(rng, amount, total, most, slope):
    if amount == 2:
        one = jax.random.randint(rng, (), max(1, total - most), min(most, total - 1) + 1)
        return jnp.stack([one, total - one])
    tallies = jnp.asarray(split_up(amount, total, most, slope), jnp.int32)
    couples = (amount - 1) // 2
    giver, receiver = tallies[1:1 + 2 * couples:2], tallies[2:2 + 2 * couples:2]
    slack = jnp.minimum(giver - 1, most - receiver)
    passed = jax.random.randint(jax.random.fold_in(rng, 1), (couples,), 0, 1 << 20) % (slack + 1)
    tallies = tallies.at[1:1 + 2 * couples:2].set(giver - passed).at[2:2 + 2 * couples:2].set(receiver + passed)
    return tallies[jax.random.permutation(jax.random.fold_in(rng, 2), amount)]


def gaussian(stream_key, shape, spread, bound, shards=(), kind=jnp.bfloat16):
    drawn = jax.random.normal(stream_key, shape, jnp.float32) * spread
    if len(shards) > 0:
        drawn = block_levels(stream_key, shape, shards, -0.22, 0.18) * drawn
    return jnp.clip(drawn, min=-bound, max=bound).astype(kind)


def bell_draw_with(own_key, extent, deviation, most, pieces, heavy, kind=jnp.bfloat16):
    values = deviation * jax.random.normal(own_key, extent, jnp.float32)
    if pieces:
        values = values * block_levels(own_key, extent, pieces, -0.22, 0.18)
    return jnp.clip(with_spikes(values, jax.random.fold_in(own_key, 3), *heavy), -most, most).astype(kind)


def setup_inputs(seed: int = 0) -> dict:
    key_of = jax.random.split(jax.random.key(seed), 13)
    inputs = bell_draw_with(key_of[0], (MICRO, ROWS, ROW_LEN, D), 1.0, 6.0, ((1, 32),), (1, 3, 32, 2.75))
    cotangent = bell_draw_with(key_of[1], (MICRO, ROWS, ROW_LEN, D), 1.0, 6.0, ((1, 32),), (1, 3, 32, 2.75))
    doc_ids = jax.vmap(lambda own: jnp.searchsorted(jnp.cumsum(uneven_parts(own, DOCS, ROW_LEN, DOC_MOST, 1)), jnp.arange(ROW_LEN), side="right"))(jax.random.split(key_of[2], MICRO * ROWS)).reshape((MICRO, ROWS, ROW_LEN)).astype(jnp.int32)
    attention_weights = draw_attention_weights(jax.random.fold_in(key_of[12], 71), 0)
    attention_momentum = gaussian(key_of[4], (4, D, D), (TOKENS ** 0.5), 1024.0, ((1, 32),), jnp.float32)
    attention_average = draw_attention_average(jax.random.fold_in(key_of[12], 71), 0)
    feedforward_weights = draw_feedforward_weights(jax.random.fold_in(key_of[12], 71), 0)
    feedforward_momentum = gaussian(key_of[7], (2, D, FF), (TOKENS ** 0.5), 1024.0, ((1, 32),), jnp.float32)
    feedforward_average = draw_feedforward_average(jax.random.fold_in(key_of[12], 71), 0)
    vector_weights = draw_vector_weights(jax.random.fold_in(key_of[12], 71), 0)
    vector_momentum = gaussian(key_of[10], (NV, D), (TOKENS ** 0.5), 1024.0, ((1, 32),), jnp.float32)
    vector_average = draw_vector_average(jax.random.fold_in(key_of[12], 71), 0)
    return dict(inputs=inputs, cotangent=cotangent, doc_ids=doc_ids, attention_weights=attention_weights, attention_momentum=attention_momentum, attention_average=attention_average, feedforward_weights=feedforward_weights, feedforward_momentum=feedforward_momentum, feedforward_average=feedforward_average, vector_weights=vector_weights, vector_momentum=vector_momentum, vector_average=vector_average)


@jax.custom_vjp
def low(v):
    return lax.optimization_barrier(v.astype(jnp.bfloat16)).astype(jnp.float32)

@jax.custom_vjp
def low_back(v):
    return v

def low_keep(v):
    return (low(v), None)

def low_pass(kept, grad):
    return (grad,)

def back_keep(v):
    return (v, None)

def back_low(kept, grad):
    return (low(grad),)
low.defvjp(low_keep, low_pass)
low_back.defvjp(back_keep, back_low)
EPSILON = 1e-12
SCALING = 0.125
MASKED = -1000000000.0
MOMENTUM = 0.5
DECAY = 0.5

def highest(left, right):
    return jnp.dot(left, right, precision=lax.Precision.HIGHEST)

def layer_norm(summed, gain_row, shift_row):
    average = lax.optimization_barrier(jnp.mean(summed, axis=-1, keepdims=True))
    centered = summed - average
    variance = lax.optimization_barrier(jnp.mean(centered * centered, axis=-1, keepdims=True))
    return centered * lax.rsqrt(variance + EPSILON) * gain_row + shift_row

def sublayer(inputs_row, attention_full, feedforward_full, vector_full, document_row, heads_used):
    head_width = heads_used * HEAD_DIM
    hidden_used = FF * heads_used // HEADS
    blocks = FF // D
    length = inputs_row.shape[0]
    attention_slab = low(attention_full[:, :, :head_width])
    feedforward_slab = low(feedforward_full[:, :, :hidden_used])
    vector_slab = low(vector_full)
    queries = low(low_back(highest(inputs_row, attention_slab[0]) + vector_slab[0, :head_width]))
    keys_all = low(low_back(highest(inputs_row, attention_slab[1])))
    values_all = low(low_back(highest(inputs_row, attention_slab[2]) + vector_slab[1, :head_width]))
    query_heads = queries.reshape(length, heads_used, HEAD_DIM)
    key_heads = keys_all.reshape(length, heads_used, HEAD_DIM)
    value_heads = values_all.reshape(length, heads_used, HEAD_DIM)
    scores = low_back(jnp.einsum('qhd,khd->hqk', query_heads, key_heads, precision=lax.Precision.HIGHEST) * SCALING)
    same_document = document_row[:, None] == document_row[None, :]
    scores = jnp.where(same_document[None], scores, MASKED)
    probability = jax.nn.softmax(scores, axis=-1)
    attended = jnp.einsum('hqk,khd->qhd', low(probability), value_heads, precision=lax.Precision.HIGHEST)
    attended = low(low_back(attended.reshape(length, head_width)))
    branch = low_back(highest(attended, attention_slab[3].T) + vector_slab[2])
    first_norm = layer_norm(inputs_row + branch, vector_slab[blocks + 4], vector_slab[blocks + 5])
    hidden_bias = vector_slab[3:3 + blocks].reshape(blocks * D)[:hidden_used]
    hidden_pre = low_back(highest(low(first_norm), feedforward_slab[0]) + hidden_bias)
    hidden = low(jax.nn.gelu(hidden_pre, approximate=False))
    second = low_back(highest(hidden, feedforward_slab[1].T) + vector_slab[3 + blocks])
    return layer_norm(first_norm + second, vector_slab[blocks + 6], vector_slab[blocks + 7])

def update(weights_now, momentum_now, average_now, gradient, rate):
    momentum_next = MOMENTUM * momentum_now + gradient
    weights_next = weights_now - rate * (gradient + MOMENTUM * momentum_next)
    average_next = DECAY * average_now + (1.0 - DECAY) * weights_next
    return (weights_next, momentum_next, average_next, weights_next.astype(jnp.bfloat16))

def reference(inputs, cotangent, doc_ids, attention_weights, attention_momentum, attention_average, feedforward_weights, feedforward_momentum, feedforward_average, vector_weights, vector_momentum, vector_average):
    row_inputs = inputs.astype(jnp.float32).reshape(MICRO * ROWS, ROW_LEN, D)
    row_cotangents = cotangent.astype(jnp.float32).reshape(MICRO * ROWS, ROW_LEN, D)
    row_documents = doc_ids.reshape(MICRO * ROWS, ROW_LEN)

    def one_row(carry, row_data):
        inputs_row, cotangent_row, document_row = row_data
        attention_grad, feedforward_grad, vector_grad = carry
        input_total = jnp.zeros((ROW_LEN, D), jnp.float32)
        full_output = input_total
        for quarter in (4, 3, 2, 1):
            heads_used = HEADS * quarter // 4
            forward = partial(sublayer, document_row=document_row, heads_used=heads_used)
            result, pullback = jax.vjp(forward, inputs_row, attention_weights, feedforward_weights, vector_weights)
            grad_input, grad_attention, grad_feedforward, grad_vector = pullback(cotangent_row)
            input_total = input_total + grad_input
            attention_grad = attention_grad + grad_attention
            feedforward_grad = feedforward_grad + grad_feedforward
            vector_grad = vector_grad + grad_vector
            if quarter == 4:
                full_output = result
        return ((attention_grad, feedforward_grad, vector_grad), (full_output.astype(jnp.bfloat16), input_total.astype(jnp.bfloat16)))
    start = (jnp.zeros_like(attention_weights), jnp.zeros_like(feedforward_weights), jnp.zeros_like(vector_weights))
    totals, stacked = lax.scan(one_row, start, (row_inputs, row_cotangents, row_documents))
    layer_out = stacked[0].reshape(MICRO, ROWS, ROW_LEN, D)
    input_grad = stacked[1].reshape(MICRO, ROWS, ROW_LEN, D)
    rate = 0.05 / math.sqrt(TOKENS)
    attention_out = update(attention_weights, attention_momentum, attention_average, totals[0], rate)
    feedforward_out = update(feedforward_weights, feedforward_momentum, feedforward_average, totals[1], rate)
    vector_out = update(vector_weights, vector_momentum, vector_average, totals[2], rate)
    return (layer_out, input_grad, attention_out[0], attention_out[1], attention_out[2], attention_out[3], feedforward_out[0], feedforward_out[1], feedforward_out[2], feedforward_out[3], vector_out[0], vector_out[1], vector_out[2], vector_out[3])
```

```python
from functools import partial
import math

import jax
import jax.numpy as jnp
from jax import lax
from jax.experimental import pallas as pl
from jax.experimental.pallas import tpu as pltpu
from jax.sharding import PartitionSpec as P

D = 768
HEADS = 12
HEAD_DIM = 64
FF = 3072
SLICES = FF // D
PAIRS = HEADS // 2
HALF = 256
WINDOW = 384

EPSILON = 1e-12
SCALING = 0.125
MASKED = -1000000000.0
MOMENTUM = 0.5
DECAY = 0.5
BF = jnp.bfloat16
F32 = jnp.float32

VMEM_LIMIT = 60 * 1024 * 1024


def dot(left, right):
    return lax.dot_general(left, right, (((1,), (0,)), ((), ())), preferred_element_type=F32)


def dot_last(left, right):
    return lax.dot_general(left, right, (((1,), (1,)), ((), ())), preferred_element_type=F32)


def dot_first(left, right):
    return lax.dot_general(left, right, (((0,), (0,)), ((), ())), preferred_element_type=F32)


def whole(shape):
    zeros = (0,) * len(shape)
    return pl.BlockSpec(shape, lambda *_: zeros, pipeline_mode=pl.Buffered(1))


def params():
    return pltpu.CompilerParams(vmem_limit_bytes=VMEM_LIMIT)


PIECES = 8
UNITS = 16
UNIT = D // UNITS
OWN = UNIT // 2
HALF_D = D // 2
NARROW = 128


def load(pieces, place_ref, moves, semaphore):
    for own in (True, False):
        for turn in range(4):
            piece = pieces[turn if own else 4 + turn]
            for index in range(4):
                start = pl.multiple_of(place_ref[4 * turn + index] * UNIT, UNIT)
                for lane, lanes, target in moves:
                    pltpu.make_async_copy(
                        piece.at[index, :, lane : lane + lanes],
                        target(own).at[pl.ds(start, UNIT), :],
                        semaphore,
                    ).start()


def all_arrived(ref, semaphore):
    pltpu.make_async_copy(ref, ref, semaphore).wait()


def cost(flops, size):
    return pl.CostEstimate(flops=int(flops), bytes_accessed=int(size), transcendentals=0)


def attention_forward_kernel(place_ref, x_ref, column_ref, row_ref, *refs):
    pieces, refs = refs[:PIECES], refs[PIECES:]
    q_ref, k_ref, v_ref, o_ref, p_ref, weights_ref, vector_ref, table_ref, semaphore = refs

    @pl.when(pl.program_id(0) == 0)
    def _():
        core = place_ref[UNITS]

        def half(own):
            which = core if own else 1 - core
            return weights_ref.at[1, :, pl.ds(pl.multiple_of(HALF_D * which, NARROW), HALF_D)]

        load(
            pieces,
            place_ref,
            (
                (0, D, lambda own: weights_ref.at[2 * (core if own else 1 - core)]),
                (D, HALF_D, half),
            ),
            semaphore.at[0],
        )
        for turn in range(4):
            pltpu.make_async_copy(
                pieces[turn].at[:, :, D + HALF_D : D + HALF_D + NARROW],
                table_ref.at[pl.ds(4 * turn, 4)],
                semaphore.at[1],
            ).start()
        all_arrived(table_ref, semaphore.at[1])
        vector = jnp.zeros((16, D), F32)
        for slot in range(UNITS):
            unit = table_ref[slot].astype(F32)
            for one in range(2):
                part = unit[OWN * one : OWN * one + 16]
                wide = jnp.concatenate([part, jnp.zeros((16, D - NARROW), F32)], axis=1)
                vector = vector + pltpu.roll(wide, UNIT * place_ref[slot] + OWN * one, 1)
        vector_ref[...] = vector
        all_arrived(weights_ref, semaphore.at[0])

    rows = x_ref[0]
    queries = (dot(rows, weights_ref[0]) + vector_ref[0:1, :]).astype(BF)
    q_ref[0] = queries * jnp.asarray(SCALING, BF)
    k_ref[0] = dot(rows, weights_ref[1]).astype(BF)
    v_ref[0] = (dot(rows, weights_ref[2]) + vector_ref[1:2, :]).astype(BF)
    length = rows.shape[0]
    lane = lax.broadcasted_iota(jnp.int32, (length, 128), 1)
    masks = [
        column_ref[0, HALF * part : HALF * (part + 1), :]
        == row_ref[0, :, 128 * part : 128 * part + WINDOW]
        for part in range(2)
    ]
    for pair in range(PAIRS):
        cols = slice(128 * pair, 128 * (pair + 1))
        q_pair = q_ref[0, :, cols]
        k_pair = k_ref[0, :, cols]
        v_pair = v_ref[0, :, cols]
        results = []
        for side in range(2):
            q_one = jnp.where((lane >= 64) == bool(side), q_pair, jnp.zeros_like(q_pair))
            parts = []
            for part in range(2):
                window = slice(128 * part, 128 * part + WINDOW)
                scores = dot_last(q_one[HALF * part : HALF * (part + 1)], k_pair[window])
                scores = jnp.where(masks[part], scores, MASKED)
                peak = jnp.max(scores, axis=-1, keepdims=True)
                exponent = jnp.exp(scores - peak)
                total = jnp.sum(exponent, axis=-1, keepdims=True)
                low = (exponent * (1.0 / total)).astype(BF)
                p_ref[0, 2 * pair + side, part] = low
                parts.append(dot(low, v_pair[window]))
            results.append(jnp.concatenate(parts, axis=0))
        o_ref[0, :, cols] = jnp.where(lane >= 64, results[1], results[0]).astype(BF)


def attention_forward(inputs, documents, place, pieces):
    micro, length, _ = inputs.shape
    block = pl.BlockSpec((1, length, D), lambda i: (i, 0, 0))
    shape = jax.ShapeDtypeStruct((micro, length, D), BF)
    return pl.pallas_call(
        attention_forward_kernel,
        grid=(micro,),
        in_specs=[
            pl.BlockSpec(memory_space=pltpu.SMEM),
            block,
            pl.BlockSpec((1, length, 1), lambda i: (i, 0, 0)),
            pl.BlockSpec((1, 1, length), lambda i: (i, 0, 0)),
        ]
        + [pl.BlockSpec(memory_space=pl.ANY)] * PIECES,
        out_specs=[block] * 4
        + [
            pl.BlockSpec((1, HEADS, 2, HALF, WINDOW), lambda i: (i, 0, 0, 0, 0)),
            whole((3, D, D)),
            whole((16, D)),
        ],
        out_shape=[shape] * 4
        + [
            jax.ShapeDtypeStruct((micro, HEADS, 2, HALF, WINDOW), BF),
            jax.ShapeDtypeStruct((3, D, D), BF),
            jax.ShapeDtypeStruct((16, D), F32),
        ],
        scratch_shapes=[pltpu.VMEM((UNITS, UNIT, NARROW), BF), pltpu.SemaphoreType.DMA((2,))],
        cost_estimate=cost(18e9, 20e6),
        compiler_params=params(),
        name="attention_forward",
    )(place, inputs, documents[:, :, None], documents[:, None, :], *pieces)


def gelu_terms(pre):
    size = jnp.abs(pre)
    scale = 1.0 / (1.0 + 0.23164188 * size)
    bell = jnp.exp(pre * pre * -0.5)
    tail = scale * (
        0.127414796
        + scale * (-0.142248368 + scale * (0.7107068705 + scale * (-0.7265760135 + scale * 0.5307027145)))
    )
    tail = tail * bell
    below = jnp.where(pre < 0.0, tail, 1.0 - tail)
    return pre * below, below + pre * bell * 0.3989422804014327


def mean_of(value):
    return jnp.sum(value, axis=-1, keepdims=True) * (1.0 / D)


def norm_forward(summed):
    centered = summed - mean_of(summed)
    inverse = lax.rsqrt(mean_of(centered * centered) + EPSILON)
    return centered * inverse, inverse


def norm_backward(scaled, normed, inverse):
    return inverse * (scaled - mean_of(scaled) - normed * mean_of(scaled * normed))


def ffn_kernel(quarter, first, layout, *refs):
    refs = list(refs)
    place_ref, x_ref, o_ref, cotangent_ref, vector_ref = refs[:5]
    refs = refs[5:]
    if not first:
        wo_ref, refs = refs[0], refs[1:]
    chunks, refs = refs[: PIECES * len(layout)], refs[PIECES * len(layout) :]
    if not first:
        before_ref, vg_before_ref = refs[:2]
        refs = refs[2:]
    x1_ref, dm_ref, g_ref, du_ref, da_ref, dh1_ref, vg_ref = refs[:7]
    refs = refs[7:]
    if quarter == SLICES:
        out_ref = refs[0]
        refs = refs[1:]
    if first:
        wo_ref, refs = refs[0], refs[1:]
    slope_ref, weights_ref, semaphore = refs

    @pl.when(pl.program_id(0) == 0)
    def _():
        core = place_ref[UNITS]

        def half(own):
            which = core if own else 1 - core
            return wo_ref.at[:, pl.ds(pl.multiple_of(HALF_D * which, NARROW), HALF_D)]

        for index, (slices, lane) in enumerate(layout):
            pieces = chunks[PIECES * index : PIECES * (index + 1)]
            if index == 0 and first:
                load(pieces, place_ref, ((0, HALF_D, half),), semaphore.at[SLICES])
            for turn, which in enumerate(slices):
                if which < quarter:
                    load(
                        pieces,
                        place_ref,
                        (
                            (
                                lane + D * turn,
                                D,
                                lambda own, which=which: weights_ref.at[which, core if own else 1 - core],
                            ),
                        ),
                        semaphore.at[which],
                    )
        if first:
            vg_ref[...] = jnp.zeros_like(vg_ref)
        else:
            vg_ref[...] = vg_before_ref[...]

    def arrived(index):
        @pl.when(pl.program_id(0) == 0)
        def _():
            all_arrived(weights_ref.at[index], semaphore.at[index])

    def vector(index):
        return vector_ref[index : index + 1, :]

    def add_row(index, value):
        vg_ref[index : index + 1, :] += jnp.sum(value, axis=0, keepdims=True)

    if first:

        @pl.when(pl.program_id(0) == 0)
        def _():
            all_arrived(wo_ref, semaphore.at[SLICES])

    width = 192 * quarter
    padded = -(-width // 128) * 128
    attended = o_ref[:, :padded]
    if padded != width:
        lane = lax.broadcasted_iota(jnp.int32, attended.shape, 1)
        attended = jnp.where(lane < width, attended, jnp.zeros_like(attended))
    branch = dot_last(attended, wo_ref[:, :padded]) + vector(2)
    normed_one, inverse_one = norm_forward(x_ref[...].astype(F32) + branch)
    first_norm = normed_one * vector(8) + vector(9)
    low = first_norm.astype(BF)
    x1_ref[...] = low
    total = first_norm + vector(7)
    for index in range(quarter):
        cols = slice(D * index, D * (index + 1))
        arrived(index)
        pre = dot(low, weights_ref[index, 0]) + vector(3 + index)
        value, slope = gelu_terms(pre)
        value = value.astype(BF)
        g_ref[:, cols] = value
        slope_ref[:, cols] = slope
        total = total + dot_last(value, weights_ref[index, 1])
    normed_two, inverse_two = norm_forward(total)
    upstream = cotangent_ref[...].astype(F32)
    if quarter == SLICES:
        out_ref[...] = (normed_two * vector(10) + vector(11)).astype(BF)
    add_row(11, upstream)
    add_row(10, upstream * normed_two)
    grad = norm_backward(upstream * vector(10), normed_two, inverse_two)
    low = grad.astype(BF)
    dm_ref[...] = low
    add_row(7, low.astype(F32))
    for index in range(quarter):
        cols = slice(D * index, D * (index + 1))
        pre = (dot(low, weights_ref[index, 1]) * slope_ref[:, cols]).astype(BF)
        du_ref[:, cols] = pre
        add_row(3 + index, pre.astype(F32))
        grad = grad + dot_last(pre, weights_ref[index, 0])
    add_row(9, grad)
    add_row(8, grad * normed_one)
    grad = norm_backward(grad * vector(8), normed_one, inverse_one)
    low = grad.astype(BF)
    da_ref[...] = low
    add_row(2, low.astype(F32))
    if first:
        dh1_ref[...] = grad
    else:
        dh1_ref[...] = before_ref[...] + grad


def ffn(quarter, place, inputs, attended, cotangent, vector, wo, chunks, before, block=512):
    tokens = inputs.shape[0]
    hidden = D * quarter
    rows = pl.BlockSpec((block, D), lambda i: (i, 0))
    wide = pl.BlockSpec((block, hidden), lambda i: (i, 0))
    first = wo is None
    low = jax.ShapeDtypeStruct((tokens, D), BF)
    low_wide = jax.ShapeDtypeStruct((tokens, hidden), BF)
    anywhere = pl.BlockSpec(memory_space=pl.ANY)
    chunks = [chunk for chunk in chunks if min(chunk[1]) < quarter]
    in_specs = [pl.BlockSpec(memory_space=pltpu.SMEM), rows, rows, rows, whole((16, D))]
    args = [place, inputs, attended, cotangent, vector]
    if not first:
        in_specs.append(whole((D, D)))
        args.append(wo)
    for chunk in chunks:
        in_specs += [anywhere] * PIECES
        args += list(chunk[0])
    if not first:
        in_specs += [rows, whole((16, D))]
        args += list(before)
    out_specs = [rows, rows, wide, wide, rows, rows, whole((16, D))]
    out_shape = [
        low,
        low,
        low_wide,
        low_wide,
        low,
        jax.ShapeDtypeStruct((tokens, D), F32),
        jax.ShapeDtypeStruct((16, D), F32),
    ]
    if quarter == SLICES:
        out_specs.append(rows)
        out_shape.append(low)
    if first:
        out_specs.append(whole((D, D)))
        out_shape.append(jax.ShapeDtypeStruct((D, D), BF))
    layout = [(chunk[1], chunk[2]) for chunk in chunks]
    return pl.pallas_call(
        partial(ffn_kernel, quarter, first, layout),
        grid=(tokens // block,),
        in_specs=in_specs,
        out_specs=out_specs,
        out_shape=out_shape,
        scratch_shapes=[
            pltpu.VMEM((block, hidden), F32),
            pltpu.VMEM((quarter, 2, D, D), BF),
            pltpu.SemaphoreType.DMA((SLICES + 1,)),
        ],
        compiler_params=params(),
        cost_estimate=cost(8e9 + quarter * 9e9, 20e6),
        name=f"ffn_{quarter}",
    )(*args)


def share(total_ref, place_ref, send_ref, keep_ref, lanes):
    core = place_ref[UNITS]
    for slot in range(UNITS):
        start = UNIT * place_ref[slot]
        other = total_ref[pl.ds(pl.multiple_of(start + OWN * (1 - core), 8), OWN), :]
        send_ref[slot, :, lanes] = other.astype(BF)
        keep_ref[slot, :, lanes] = total_ref[pl.ds(pl.multiple_of(start + OWN * core, 8), OWN), :]


def ffn_gradient_kernel(count, steps, *refs):
    place_ref, refs = refs[0], refs[1:]
    inputs, refs = refs[: 4 * count], refs[4 * count :]
    send_ref, keep_ref, up_ref, down_ref = refs
    step = pl.program_id(0)

    @pl.when(step == 0)
    def _():
        up_ref[...] = jnp.zeros_like(up_ref)
        down_ref[...] = jnp.zeros_like(down_ref)

    for index in range(count):
        x1_ref, dm_ref, g_ref, du_ref = inputs[4 * index : 4 * index + 4]

        @pl.when(step // steps == index)
        def _():
            up_ref[...] += dot_first(x1_ref[...], du_ref[...])
            down_ref[...] += dot_first(dm_ref[...], g_ref[...])

    @pl.when(step == count * steps - 1)
    def _():
        for index, ref in enumerate((up_ref, down_ref)):
            share(ref, place_ref, send_ref, keep_ref, slice(D * index, D * (index + 1)))


def ffn_gradient(column, place, states, block=512):
    tokens = states[0][0].shape[0]
    steps = tokens // block
    count = len(states)
    in_specs, args = [pl.BlockSpec(memory_space=pltpu.SMEM)], [place]
    for index, state in enumerate(states):
        def narrow(i, index=index):
            return (jnp.clip(i - index * steps, 0, steps - 1), 0)

        def wide(i, index=index):
            return (jnp.clip(i - index * steps, 0, steps - 1), column)

        in_specs += [
            pl.BlockSpec((block, D), narrow),
            pl.BlockSpec((block, D), narrow),
            pl.BlockSpec((block, D), wide),
            pl.BlockSpec((block, D), wide),
        ]
        args += list(state)
    return pl.pallas_call(
        partial(ffn_gradient_kernel, count, steps),
        grid=(count * steps,),
        in_specs=in_specs,
        out_specs=[whole((UNITS, OWN, 2 * D))] * 2,
        out_shape=[
            jax.ShapeDtypeStruct((UNITS, OWN, 2 * D), BF),
            jax.ShapeDtypeStruct((UNITS, OWN, 2 * D), F32),
        ],
        scratch_shapes=[pltpu.VMEM((D, D), F32)] * 2,
        cost_estimate=cost(count * 5e9, 20e6),
        compiler_params=params(),
        name=f"ffn_gradient_{column}",
    )(*args)


def attention_backward_kernel(
    place_ref, x_ref, q_ref, k_ref, v_ref, o_ref, p_ref, da4_ref, da3_ref, da2_ref, da1_ref, dh1_ref, weights_ref, wo_ref,
    vg_ref, *refs
):
    (
        dx_ref, send_ref, keep_ref, dw_ref, table_ref, do_ref, sum_ref, dq_ref, dk_ref, dv_ref,
    ) = refs

    @pl.when(pl.program_id(0) == 0)
    def _():
        dw_ref[...] = jnp.zeros_like(dw_ref)
        table_ref[...] = vg_ref[...]

    length = x_ref.shape[1]
    running = da4_ref[0].astype(F32)
    sum_ref[3] = da4_ref[0]
    for index, ref in ((2, da3_ref), (1, da2_ref), (0, da1_ref)):
        running = running + ref[0].astype(F32)
        sum_ref[index] = running.astype(BF)
    lane = lax.broadcasted_iota(jnp.int32, (length, 256), 1)
    for block in range(3):
        cols = slice(256 * block, 256 * (block + 1))
        edge = 192 * (block + 1) - 256 * block
        do_ref[:, cols] = jnp.where(
            lane < edge,
            dot(sum_ref[block], wo_ref[:, cols]),
            dot(sum_ref[block + 1], wo_ref[:, cols]),
        ).astype(BF)
        attended = o_ref[0, :, cols]
        nothing = jnp.zeros_like(attended)
        dw_ref[3, :, cols] += dot_first(
            sum_ref[block], jnp.where(lane < edge, attended, nothing)
        ) + dot_first(sum_ref[block + 1], jnp.where(lane < edge, nothing, attended))
    lane = lax.broadcasted_iota(jnp.int32, (length, 128), 1)
    dv_ref[...] = jnp.zeros_like(dv_ref)
    dk_ref[...] = jnp.zeros_like(dk_ref)
    for pair in range(PAIRS):
        cols = slice(128 * pair, 128 * (pair + 1))
        q_pair = q_ref[0, :, cols]
        k_pair = k_ref[0, :, cols]
        v_pair = v_ref[0, :, cols]
        do_pair = do_ref[:, cols]
        q_turned = q_pair.T
        do_turned = do_pair.T
        results = []
        for side in range(2):
            do_one = jnp.where((lane >= 64) == bool(side), do_pair, jnp.zeros_like(do_pair))
            heads = slice(64 * side, 64 * (side + 1))
            out = slice(128 * pair + 64 * side, 128 * pair + 64 * (side + 1))
            parts = []
            for part in range(2):
                window = slice(128 * part, 128 * part + WINDOW)
                rows = slice(HALF * part, HALF * (part + 1))
                low = p_ref[0, 2 * pair + side, part]
                dp = dot_last(do_one[rows], v_pair[window])
                prob = low.astype(F32)
                mixed = prob * dp
                ds = (mixed - prob * jnp.sum(mixed, axis=-1, keepdims=True)).astype(BF)
                dv_ref[out, window] += dot(do_turned[heads, rows], low)
                dk_ref[out, window] += dot(q_turned[heads, rows], ds)
                parts.append(dot(ds, k_pair[window]))
            results.append(jnp.concatenate(parts, axis=0))
        dq_ref[:, cols] = (jnp.where(lane >= 64, results[1], results[0]) * SCALING).astype(BF)
    dq = dq_ref[...]
    dk = dk_ref[...].astype(BF).T
    dv = dv_ref[...].astype(BF).T
    dx_ref[0] = (
        dh1_ref[0]
        + dot_last(dq, weights_ref[0])
        + dot_last(dk, weights_ref[1])
        + dot_last(dv, weights_ref[2])
    ).astype(BF)
    turned = x_ref[0].T
    dw_ref[0] += dot(turned, dq)
    dw_ref[1] += dot(turned, dk)
    dw_ref[2] += dot(turned, dv)
    table_ref[0:1, :] += jnp.sum(dq.astype(F32), axis=0, keepdims=True)
    table_ref[1:2, :] += jnp.sum(dv.astype(F32), axis=0, keepdims=True)

    @pl.when(pl.program_id(0) == pl.num_programs(0) - 1)
    def _():
        for index in range(4):
            share(dw_ref.at[index], place_ref, send_ref, keep_ref, slice(D * index, D * (index + 1)))
        core = place_ref[UNITS]
        lanes = slice(4 * D, 4 * D + NARROW)
        table = table_ref[...]
        nothing = jnp.zeros((OWN - table.shape[0], NARROW), F32)
        for slot in range(UNITS):
            for one, ref in ((1 - core, send_ref), (core, keep_ref)):
                turned = pltpu.roll(table, lax.rem(D - UNIT * place_ref[slot] - OWN * one, D), 1)[:, :NARROW]
                ref[slot, :, lanes] = jnp.concatenate([turned, nothing], axis=0).astype(ref.dtype)


def attention_backward(place, inputs, q, k, v, o, p, das, dh1, weights, wo, table):
    micro, length, _ = inputs.shape
    block = pl.BlockSpec((1, length, D), lambda i: (i, 0, 0))
    lanes = 4 * D + NARROW
    return pl.pallas_call(
        attention_backward_kernel,
        grid=(micro,),
        in_specs=[pl.BlockSpec(memory_space=pltpu.SMEM)]
        + [block] * 5
        + [pl.BlockSpec((1, HEADS, 2, HALF, WINDOW), lambda i: (i, 0, 0, 0, 0))]
        + [block] * 5
        + [whole((3, D, D)), whole((D, D)), whole((16, D))],
        out_specs=[block, whole((UNITS, OWN, lanes)), whole((UNITS, OWN, lanes))],
        out_shape=[
            jax.ShapeDtypeStruct((micro, length, D), BF),
            jax.ShapeDtypeStruct((UNITS, OWN, lanes), BF),
            jax.ShapeDtypeStruct((UNITS, OWN, lanes), F32),
        ],
        scratch_shapes=[
            pltpu.VMEM((4, D, D), F32),
            pltpu.VMEM((16, D), F32),
            pltpu.VMEM((length, D), BF),
            pltpu.VMEM((4, length, D), BF),
            pltpu.VMEM((length, D), BF),
            pltpu.VMEM((D, length), F32),
            pltpu.VMEM((D, length), F32),
        ],
        compiler_params=params(),
        cost_estimate=cost(40e9, 30e6),
        name="attention_backward",
    )(place, inputs, q, k, v, o, p, *das, dh1, weights, wo, table)


AXES = ("wide", "narrow")
PLANE = (0, 4, 2, 6)
ALONG = (0, 8, 16, 24)
DEVICES = 32


def flip(value, bits):
    return lax.ppermute(value, AXES, [(device, device ^ bits) for device in range(DEVICES)])


def tie(value, *earlier):
    return lax.optimization_barrier((value, *earlier))[0] if earlier else value


class Gather:
    def __init__(self, parts, core):
        mine = jnp.where(core == 0, parts[0], parts[1])
        theirs = flip(jnp.where(core == 0, parts[1], parts[0]), 1)
        self.unit = jnp.where(core == 0, jnp.concatenate([mine, theirs]), jnp.concatenate([theirs, mine]))

    def along(self, *earlier):
        self.unit = tie(self.unit, *earlier)
        self.near = jnp.stack([self.unit if bits == 0 else flip(self.unit, bits) for bits in ALONG])

    def plane(self, *earlier):
        self.near = tie(self.near, *earlier)
        self.own = [self.near if bits == 0 else flip(self.near, bits) for bits in PLANE]

    def peers(self, *earlier):
        own = [tie(piece, *earlier) for piece in self.own]
        self.peer = [flip(piece, 1) for piece in own]
        return self.own + self.peer


def gather_plain(parts):
    full = [lax.all_gather(part, AXES, axis=0, tiled=True).reshape(UNITS, UNIT, -1) for part in parts]
    return [value[4 * turn : 4 * turn + 4] for value in full for turn in range(4)]


class Reduce:
    def __init__(self, send, keep):
        self.keep = keep
        self.out = [send]
        self.arrived = [flip(send, 1)]

    def wait(self, earlier):
        if earlier:
            self.arrived = list(lax.optimization_barrier((*self.arrived, *earlier)))[: len(self.arrived)]

    def plane(self, *earlier):
        self.wait(earlier)

        def piece(turn):
            part = slice(4 * turn, 4 * turn + 4)
            return self.keep[part] + self.arrived[0][part].astype(F32)

        self.out = [piece(turn).astype(BF) for turn in (1, 2, 3)]
        self.total = piece(0)
        self.arrived = [flip(value, bits) for value, bits in zip(self.out, PLANE[1:])]

    def along(self, *earlier):
        self.wait(earlier)
        total = self.total
        for value in self.arrived:
            total = total + value.astype(F32)
        self.out = [total[turn].astype(BF) for turn in (1, 2, 3)]
        self.total = total[0]
        self.arrived = [flip(value, bits) for value, bits in zip(self.out, ALONG[1:])]

    def result(self, *earlier):
        self.wait(earlier)
        total = self.total
        for value in self.arrived:
            total = total + value.astype(F32)
        return total


class ReducePlain:
    def __init__(self, send, keep):
        self.send, self.keep, self.out = send, keep, [send]

    def plane(self, *earlier):
        pass

    along = plane

    def result(self, *earlier):
        both = jnp.stack([self.keep.astype(BF), self.send], axis=1).reshape(D, -1)
        return lax.psum_scatter(both, AXES, scatter_dimension=0, tiled=True).astype(F32)


def update(weights_now, momentum_now, average_now, gradient, rate):
    momentum_next = MOMENTUM * momentum_now + gradient
    weights_next = weights_now - rate * (gradient + MOMENTUM * momentum_next)
    average_next = DECAY * average_now + (1.0 - DECAY) * weights_next
    return (weights_next, momentum_next, average_next, weights_next.astype(BF))


def body(
    inputs,
    cotangent,
    doc_ids,
    attention_weights,
    attention_momentum,
    attention_average,
    feedforward_weights,
    feedforward_momentum,
    feedforward_average,
    vector_weights,
    vector_momentum,
    vector_average,
):
    micro, _, length, _ = inputs.shape
    count = lax.axis_size("wide") * lax.axis_size("narrow")
    me = lax.axis_index("wide") * lax.axis_size("narrow") + lax.axis_index("narrow")
    rows = attention_weights.shape[1]
    names = vector_weights.shape[0]
    paired = count == DEVICES
    if paired:
        core = me % 2
        offsets = [(plane ^ along) // 2 for plane in PLANE for along in ALONG]
        slots = me // 2 ^ jnp.asarray(offsets, jnp.int32)
    else:
        core = jnp.zeros((), jnp.int32)
        slots = jnp.arange(UNITS, dtype=jnp.int32)
    place = jnp.concatenate([slots, jnp.full((UNITS,), core, jnp.int32)])

    attention_low = attention_weights.astype(BF)
    hidden_low = feedforward_weights.astype(BF)
    vector_low = vector_weights.astype(BF)

    def halves(value):
        return value[:, :HALF_D], value[:, HALF_D:]

    def parts_of(columns):
        return [jnp.concatenate([column[which] for column in columns], axis=1) for which in (0, 1)]

    def hidden(which):
        return tuple(hidden_low[c, :, D * which : D * (which + 1)] for c in (0, 1))

    groups = ((0, 1), (2, 3))
    parts = [
        parts_of([(attention_low[0], attention_low[2]), halves(attention_low[1])]),
        parts_of([halves(attention_low[3])] + [hidden(which) for which in groups[0]]),
        parts_of([hidden(which) for which in groups[1]]),
    ]
    inputs_rows, cotangent_rows = inputs[:, 0], cotangent[:, 0]

    def flat(value):
        return value.reshape(micro * length, D)

    def split(value):
        return value.reshape(micro, length, D)

    def forward(pieces, place):
        return attention_forward(inputs_rows, doc_ids[:, 0], place, pieces)

    if paired:
        table = jnp.pad(vector_low, ((0, OWN - names), (0, NARROW - OWN)))
        parts[0] = [jnp.concatenate([part, table], axis=1) for part in parts[0]]
        one, two, three = [Gather(part, core) for part in parts]
        one.along()
        one.plane()
        first_pieces = one.peers()
        two.along(one.near)
        two.plane(*one.peer)
        three.along(two.near)
        q, k, v, o, p, weights, vector = forward(first_pieces, tie(place, two.near, three.near))
        second_pieces = two.peers(q)
        three.plane(q, *two.peer)
        ready = three.near
    else:
        table = lax.all_gather(vector_low, AXES, axis=1, tiled=True)
        table = table.reshape(names, UNITS, 2, OWN).transpose(1, 2, 0, 3)
        table = jnp.pad(table, ((0, 0), (0, 0), (0, OWN - names), (0, NARROW - OWN)))
        table = table.reshape(UNITS, UNIT, NARROW)
        first_pieces, second_pieces, third_pieces = [gather_plain(part) for part in parts]
        first_pieces = [
            jnp.concatenate([piece, table[4 * (turn % 4) : 4 * (turn % 4) + 4]], axis=2)
            for turn, piece in enumerate(first_pieces)
        ]
        q, k, v, o, p, weights, vector = forward(first_pieces, place)
        ready = place
    chunks = [(second_pieces, groups[0], HALF_D)]

    states, before, wo = {}, None, None

    def widths(quarter, *earlier):
        nonlocal before, wo
        result = ffn(
            quarter, tie(place, *earlier), flat(inputs_rows), flat(o), flat(cotangent_rows), vector, wo, chunks, before
        )
        states[quarter] = result[:5]
        before = (result[5], result[6])
        if wo is None:
            wo = result[-1]
        return result

    def gradient(which, *earlier):
        return ffn_gradient(
            which, tie(place, *earlier), [states[quarter][:4] for quarter in range(which + 1, SLICES + 1)]
        )

    reduce = Reduce if paired else ReducePlain
    widths(1, ready)
    chunks.append((three.peers(before[0]) if paired else third_pieces, groups[1], 0))
    layer_out = split(widths(4)[7])
    three = reduce(*gradient(3))
    widths(3, *three.out)
    three.plane(before[0])
    two = reduce(*gradient(2, *three.out))
    widths(2, *two.out)
    three.along(before[0])
    two.plane(before[0])
    input_grad, send, keep = attention_backward(
        tie(place, *three.out, *two.out), inputs_rows, q, k, v, o, p,
        [split(states[quarter][4]) for quarter in (4, 3, 2, 1)],
        split(before[0]), weights, wo, before[1],
    )
    attention = reduce(send, keep)
    two.along(send)
    one = reduce(*gradient(1, *attention.out, *two.out))
    last = one.out[0]
    attention.plane(last)
    zero = reduce(*gradient(0, last, *attention.out))
    last = zero.out[0]
    attention.along(last)
    one.plane(*attention.out)
    zero.plane(*one.out)
    attention_sum = attention.result(*zero.out)
    one.along(*zero.out)
    zero.along(*one.out)
    sums = [zero.result(), one.result(*zero.out), two.result(last), three.result(last)]

    attention_gradient = jnp.stack([attention_sum[:, D * c : D * (c + 1)] for c in range(4)])
    feedforward_gradient = jnp.stack(
        [jnp.concatenate([sums[s][:, D * c : D * (c + 1)] for s in range(SLICES)], axis=1) for c in (0, 1)]
    )
    if paired:
        vector_gradient = attention_sum[:names, 4 * D : 4 * D + rows]
    else:
        table = jnp.stack([keep, send.astype(F32)], axis=1)[:, :, :names, 4 * D : 4 * D + OWN]
        table = table.transpose(2, 0, 1, 3).reshape(names, D)
        vector_gradient = lax.psum_scatter(table, AXES, scatter_dimension=1, tiled=True)

    rate = 0.05 / math.sqrt(micro * length * count)
    return (
        layer_out[:, None],
        input_grad[:, None],
        *update(attention_weights, attention_momentum, attention_average, attention_gradient, rate),
        *update(feedforward_weights, feedforward_momentum, feedforward_average, feedforward_gradient, rate),
        *update(vector_weights, vector_momentum, vector_average, vector_gradient, rate),
    )


def solution(mesh):
    row = P(None, AXES, None, None)
    matrix = P(None, AXES, None)
    table = P(None, AXES)
    in_specs = (row, row, matrix) + (matrix,) * 6 + (table,) * 3
    out_specs = (row, row) + (matrix,) * 8 + (table,) * 4
    return jax.shard_map(body, mesh=mesh, in_specs=in_specs, out_specs=out_specs, check_vma=False)
```

```python
from functools import partial
import math

import jax
import jax.numpy as jnp
from jax import lax
from jax.experimental import pallas as pl
from jax.experimental.pallas import tpu as pltpu
from jax.sharding import PartitionSpec as P

D = 768
HEADS = 12
HEAD_DIM = 64
FF = 3072
SLICES = FF // D
PAIRS = HEADS // 2
HALF = 256
WINDOW = 384

EPSILON = 1e-12
SCALING = 0.125
MASKED = -1000000000.0
MOMENTUM = 0.5
DECAY = 0.5
BF = jnp.bfloat16
F32 = jnp.float32

TILE = 256
TALL = 256
VMEM_LIMIT = 60 * 1024 * 1024


def dot(left, right):
    return lax.dot_general(left, right, (((1,), (0,)), ((), ())), preferred_element_type=F32)


def dot_last(left, right):
    return lax.dot_general(left, right, (((1,), (1,)), ((), ())), preferred_element_type=F32)


def dot_first(left, right):
    return lax.dot_general(left, right, (((0,), (0,)), ((), ())), preferred_element_type=F32)


def whole(shape):
    zeros = (0,) * len(shape)
    return pl.BlockSpec(shape, lambda *_: zeros, pipeline_mode=pl.Buffered(1))


def params():
    return pltpu.CompilerParams(vmem_limit_bytes=VMEM_LIMIT)


PIECES = 8
UNITS = 16
UNIT = D // UNITS
OWN = UNIT // 2
HALF_D = D // 2
NARROW = 128


def load(pieces, place_ref, moves, semaphore):
    for own in (True, False):
        for turn in range(4):
            piece = pieces[turn if own else 4 + turn]
            for lane, lanes, target in moves:
                pltpu.make_async_copy(
                    piece.at[:, :, lane : lane + lanes],
                    target(own).at[:, place_ref[UNITS + 4 + turn]],
                    semaphore,
                ).start()


def all_arrived(ref, semaphore):
    pltpu.make_async_copy(ref, ref, semaphore).wait()


def cost(flops, size):
    return pl.CostEstimate(flops=int(flops), bytes_accessed=int(size), transcendentals=0)


def attention_forward_kernel(place_ref, x_ref, column_ref, row_ref, *refs):
    pieces, refs = refs[:PIECES], refs[PIECES:]
    q_ref, k_ref, v_ref, o_ref, p_ref, weights_ref, vector_ref, table_ref, semaphore = refs


    @pl.when(pl.program_id(0) == 0)
    def _():
        core = place_ref[UNITS]

        def half(own):
            which = core if own else 1 - core
            return weights_ref.at[1, :, :, :, pl.ds(pl.multiple_of(HALF_D * which, NARROW), HALF_D)]

        load(
            pieces,
            place_ref,
            (
                (0, D, lambda own: weights_ref.at[2 * (core if own else 1 - core)]),
                (D, HALF_D, half),
            ),
            semaphore.at[0],
        )
        for turn in range(4):
            pltpu.make_async_copy(
                pieces[turn].at[:, :, D + HALF_D : D + HALF_D + NARROW],
                table_ref.at[pl.ds(4 * turn, 4)],
                semaphore.at[1],
            ).start()
        all_arrived(table_ref, semaphore.at[1])
        vector = jnp.zeros((16, D), F32)
        for slot in range(UNITS):
            unit = table_ref[slot].astype(F32)
            for one in range(2):
                part = unit[OWN * one : OWN * one + 16]
                wide = jnp.concatenate([part, jnp.zeros((16, D - NARROW), F32)], axis=1)
                unit_number = 4 * (slot % 4) + place_ref[UNITS + 4 + slot // 4]
                vector = vector + pltpu.roll(wide, UNIT * unit_number + OWN * one, 1)
        vector_ref[...] = vector
        all_arrived(weights_ref, semaphore.at[0])

    rows = x_ref[0]
    queries = (dot(rows, weights_ref[0].reshape(D, D)) + vector_ref[0:1, :]).astype(BF)
    q_ref[0] = queries * jnp.asarray(SCALING, BF)
    k_ref[0] = dot(rows, weights_ref[1].reshape(D, D)).astype(BF)
    v_ref[0] = (dot(rows, weights_ref[2].reshape(D, D)) + vector_ref[1:2, :]).astype(BF)
    length = rows.shape[0]
    lane = lax.broadcasted_iota(jnp.int32, (length, 128), 1)
    masks = [
        column_ref[0, HALF * part : HALF * (part + 1), :]
        == row_ref[0, :, 128 * part : 128 * part + WINDOW]
        for part in range(2)
    ]
    for pair in range(PAIRS):
        cols = slice(128 * pair, 128 * (pair + 1))
        q_pair = q_ref[0, :, cols]
        k_pair = k_ref[0, :, cols]
        v_pair = v_ref[0, :, cols]
        results = []
        for side in range(2):
            q_one = jnp.where((lane >= 64) == bool(side), q_pair, jnp.zeros_like(q_pair))
            parts = []
            for part in range(2):
                window = slice(128 * part, 128 * part + WINDOW)
                scores = dot_last(q_one[HALF * part : HALF * (part + 1)], k_pair[window])
                scores = jnp.where(masks[part], scores, MASKED)
                peak = jnp.max(scores, axis=-1, keepdims=True)
                exponent = jnp.exp(scores - peak)
                total = jnp.sum(exponent, axis=-1, keepdims=True)
                low = (exponent * (1.0 / total)).astype(BF)
                p_ref[0, 2 * pair + side, part] = low
                parts.append(dot(low, v_pair[window]))
            results.append(jnp.concatenate(parts, axis=0))
        o_ref[0, :, cols] = jnp.where(lane >= 64, results[1], results[0]).astype(BF)


def attention_forward(inputs, documents, place, pieces):
    micro, length, _ = inputs.shape
    block = pl.BlockSpec((1, length, D), lambda i: (i, 0, 0))
    shape = jax.ShapeDtypeStruct((micro, length, D), BF)
    return pl.pallas_call(
        attention_forward_kernel,
        grid=(micro,),
        in_specs=[
            pl.BlockSpec(memory_space=pltpu.SMEM),
            block,
            pl.BlockSpec((1, length, 1), lambda i: (i, 0, 0)),
            pl.BlockSpec((1, 1, length), lambda i: (i, 0, 0)),
        ]
        + [pl.BlockSpec(memory_space=pl.ANY)] * PIECES,
        out_specs=[block] * 4
        + [
            pl.BlockSpec((1, HEADS, 2, HALF, WINDOW), lambda i: (i, 0, 0, 0, 0)),
            whole((3, 4, 4, UNIT, D)),
            whole((16, D)),
        ],
        out_shape=[shape] * 4
        + [
            jax.ShapeDtypeStruct((micro, HEADS, 2, HALF, WINDOW), BF),
            jax.ShapeDtypeStruct((3, 4, 4, UNIT, D), BF),
            jax.ShapeDtypeStruct((16, D), F32),
        ],
        scratch_shapes=[pltpu.VMEM((UNITS, UNIT, NARROW), BF), pltpu.SemaphoreType.DMA((2,))],
        cost_estimate=cost(18e9, 20e6),
        compiler_params=params(),
        name="attention_forward",
    )(place, inputs, documents[:, :, None], documents[:, None, :], *pieces)


def gelu_terms(pre):
    below = 0.5 + 0.5 * lax.erf(pre * math.sqrt(0.5))
    bell = jnp.exp2(pre * pre * (-0.5 * math.log2(math.e)))
    return pre * below, below + (pre * (1.0 / math.sqrt(2.0 * math.pi))) * bell


def mean_of(value):
    return jnp.sum(value, axis=-1, keepdims=True) * (1.0 / D)


def norm_forward(summed):
    centered = summed - mean_of(summed)
    inverse = lax.rsqrt(mean_of(centered * centered) + EPSILON)
    return centered * inverse, inverse


def norm_backward(scaled, normed, inverse):
    return inverse * (scaled - mean_of(scaled) - normed * mean_of(scaled * normed))


def ffn_kernel(quarter, first, layout, *refs):
    refs = list(refs)
    place_ref, x_ref, o_ref, cotangent_ref, vector_ref = refs[:5]
    refs = refs[5:]
    if not first:
        wo_ref, refs = refs[0], refs[1:]
    chunks, refs = refs[: PIECES * len(layout)], refs[PIECES * len(layout) :]
    if not first:
        before_ref, vg_before_ref = refs[:2]
        refs = refs[2:]
    x1_ref, dm_ref, g_ref, du_ref, da_ref, dh1_ref, vg_ref = refs[:7]
    refs = refs[7:]
    if quarter == SLICES:
        out_ref = refs[0]
        refs = refs[1:]
    if first:
        wo_ref, refs = refs[0], refs[1:]
    slope_ref, total_ref, weights_ref, semaphore = refs

    @pl.when(pl.program_id(0) == 0)
    def _():
        core = place_ref[UNITS]

        def half(own):
            which = core if own else 1 - core
            return wo_ref.at[:, :, :, pl.ds(pl.multiple_of(HALF_D * which, NARROW), HALF_D)]

        for index, (slices, lane) in enumerate(layout):
            pieces = chunks[PIECES * index : PIECES * (index + 1)]
            if index == 0 and first:
                load(pieces, place_ref, ((0, HALF_D, half),), semaphore.at[SLICES])
            count = min(len(slices), quarter - slices[0])
            lanes = slice(D * slices[0], D * (slices[0] + count))
            load(
                pieces,
                place_ref,
                ((lane, D * count, lambda own, lanes=lanes: weights_ref.at[core if own else 1 - core, :, :, :, lanes]),),
                semaphore.at[index],
            )
        if first:
            vg_ref[...] = jnp.zeros_like(vg_ref)
        else:
            vg_ref[...] = vg_before_ref[...]

    def arrived(index):
        @pl.when(pl.program_id(0) == 0)
        def _():
            slices = layout[index][0]
            count = min(len(slices), quarter - slices[0])
            ref = weights_ref.at[:, :, :, :, D * slices[0] : D * (slices[0] + count)]
            all_arrived(ref, semaphore.at[index])

    def vector(index):
        return vector_ref[index : index + 1, :]

    if first:

        @pl.when(pl.program_id(0) == 0)
        def _():
            all_arrived(wo_ref, semaphore.at[SLICES])

    def add_row(index, value, lanes=slice(0, D)):
        vg_ref[index : index + 1, lanes] += jnp.sum(value, axis=0, keepdims=True)

    width = 192 * quarter
    padded = -(-width // 128) * 128
    length = x_ref.shape[0]
    tops = range(0, length, TALL)
    ones, centers = {}, {}
    wo = wo_ref[...].reshape(D, D)[:, :padded]
    for top in tops:
        rows = slice(top, top + TALL)
        attended = o_ref[rows, :padded]
        if padded != width:
            lane = lax.broadcasted_iota(jnp.int32, attended.shape, 1)
            attended = jnp.where(lane < width, attended, jnp.zeros_like(attended))
        branch = dot_last(attended, wo) + vector(2)
        ones[top] = norm_forward(x_ref[rows, :].astype(F32) + branch)
        first_norm = ones[top][0] * vector(8) + vector(9)
        x1_ref[rows, :] = first_norm.astype(BF)
        total_ref[rows, :] = first_norm + vector(7)
    for index in range(quarter):
        for number, (slices, _) in enumerate(layout):
            if slices[0] == index:
                arrived(number)
        for top in range(0, length, TILE):
            for column in range(D * index, D * (index + 1), TILE):
                rows, cols = slice(top, top + TILE), slice(column, column + TILE)
                lanes = slice(column % D, column % D + TILE)
                matrix = weights_ref[0, :, :, :, cols].reshape(D, TILE)
                pre = dot(x1_ref[rows, :], matrix) + vector_ref[3 + index : 4 + index, lanes]
                value, slope = gelu_terms(pre)
                g_ref[rows, cols] = value.astype(BF)
                slope_ref[rows, cols] = slope
    down = weights_ref[1].reshape(D, D * quarter)
    for top in tops:
        rows = slice(top, top + TALL)
        normed, inverse = norm_forward(total_ref[rows, :] + dot_last(g_ref[rows, :], down))
        upstream = cotangent_ref[rows, :].astype(F32)
        if quarter == SLICES:
            out_ref[rows, :] = (normed * vector(10) + vector(11)).astype(BF)
            add_row(11, upstream * float(SLICES))
        add_row(10, upstream * normed)
        grad = norm_backward(upstream * vector(10), normed, inverse)
        low = grad.astype(BF)
        dm_ref[rows, :] = low
        add_row(7, low.astype(F32))
        total_ref[rows, :] = grad
    for index in range(quarter):
        for top in range(0, length, TILE):
            for column in range(D * index, D * (index + 1), TILE):
                rows, cols = slice(top, top + TILE), slice(column, column + TILE)
                lanes = slice(column % D, column % D + TILE)
                matrix = weights_ref[1, :, :, :, cols].reshape(D, TILE)
                pre = (dot(dm_ref[rows, :], matrix) * slope_ref[rows, cols]).astype(BF)
                du_ref[rows, cols] = pre
                add_row(3 + index, pre.astype(F32), lanes)
    up = weights_ref[0].reshape(D, D * quarter)
    for top in tops:
        rows = slice(top, top + TALL)
        normed, inverse = ones[top]
        grad = total_ref[rows, :] + dot_last(du_ref[rows, :], up)
        add_row(9, grad)
        add_row(8, grad * normed)
        grad = norm_backward(grad * vector(8), normed, inverse)
        low = grad.astype(BF)
        da_ref[rows, :] = low
        add_row(2, low.astype(F32))
        if first:
            dh1_ref[rows, :] = grad
        else:
            dh1_ref[rows, :] = before_ref[rows, :] + grad


def ffn(quarter, place, inputs, attended, cotangent, vector, wo, chunks, before, block=512):
    tokens = inputs.shape[0]
    hidden = D * quarter
    rows = pl.BlockSpec((block, D), lambda i: (i, 0))
    wide = pl.BlockSpec((block, hidden), lambda i: (i, 0))
    first = wo is None
    low = jax.ShapeDtypeStruct((tokens, D), BF)
    low_wide = jax.ShapeDtypeStruct((tokens, hidden), BF)
    anywhere = pl.BlockSpec(memory_space=pl.ANY)
    chunks = [chunk for chunk in chunks if min(chunk[1]) < quarter]
    in_specs = [pl.BlockSpec(memory_space=pltpu.SMEM), rows, rows, rows, whole((16, D))]
    args = [place, inputs, attended, cotangent, vector]
    if not first:
        in_specs.append(whole((4, 4, UNIT, D)))
        args.append(wo)
    for chunk in chunks:
        in_specs += [anywhere] * PIECES
        args += list(chunk[0])
    if not first:
        in_specs += [rows, whole((16, D))]
        args += list(before)
    out_specs = [rows, rows, wide, wide, rows, rows, whole((16, D))]
    out_shape = [
        low,
        low,
        low_wide,
        low_wide,
        low,
        jax.ShapeDtypeStruct((tokens, D), F32),
        jax.ShapeDtypeStruct((16, D), F32),
    ]
    if quarter == SLICES:
        out_specs.append(rows)
        out_shape.append(low)
    if first:
        out_specs.append(whole((4, 4, UNIT, D)))
        out_shape.append(jax.ShapeDtypeStruct((4, 4, UNIT, D), BF))
    layout = [(chunk[1], chunk[2]) for chunk in chunks]
    return pl.pallas_call(
        partial(ffn_kernel, quarter, first, layout),
        grid=(tokens // block,),
        in_specs=in_specs,
        out_specs=out_specs,
        out_shape=out_shape,
        scratch_shapes=[
            pltpu.VMEM((block, hidden), F32),
            pltpu.VMEM((block, D), F32),
            pltpu.VMEM((2, 4, 4, UNIT, hidden), BF),
            pltpu.SemaphoreType.DMA((SLICES + 1,)),
        ],
        compiler_params=params(),
        cost_estimate=cost(8e9 + quarter * 9e9, 20e6),
        name=f"ffn_{quarter}",
    )(*args)


def blocks():
    for plane in range(4):
        for along in range(4):
            start = UNIT * (4 * along + plane)
            yield plane, along, slice(start, start + UNIT)


def ffn_gradient_kernel(column, count, place_ref, *refs):
    inputs, refs = refs[: 4 * count], refs[4 * count :]
    send_ref, keep_ref, x1_ref, du_ref, dm_ref, g_ref, total_ref, semaphore, keep_semaphore = refs
    size = inputs[0].shape[0]
    cols = slice(D * column, D * (column + 1))

    def copies(index, turn):
        rows = slice(size * index, size * (index + 1))
        low, grad, value, pre = inputs[4 * index : 4 * index + 4]
        pairs = (((low, x1_ref), (pre.at[:, cols], du_ref)), ((grad, dm_ref), (value.at[:, cols], g_ref)))[turn]
        return [pltpu.make_async_copy(source, target.at[rows], semaphore.at[index, turn]) for source, target in pairs]

    def start(index, turn):
        for copy in copies(index, turn):
            copy.start()

    order = [(index, turn) for index in range(count) for turn in range(2)]
    for item in order[:1]:
        start(*item)
    for number, (index, turn) in enumerate(order):
        for copy in copies(index, turn):
            copy.wait()
        for item in order[2 * number + 1 : 2 * number + 3]:
            start(*item)
        rows = slice(size * index, size * (index + 1))
        left, right = ((x1_ref, du_ref), (dm_ref, g_ref))[turn]
        product = dot_first(left[rows, :], right[rows, :])
        if index == 0:
            total_ref[turn] = product
        else:
            total_ref[turn] += product
    core = place_ref[UNITS]
    for plane, along, rows in blocks():
        pltpu.make_async_copy(total_ref.at[core, rows], keep_ref.at[plane, along], keep_semaphore).start()
    for plane, along, rows in blocks():
        send_ref[plane, along] = total_ref[1 - core, rows, :].astype(BF)
    all_arrived(keep_ref, keep_semaphore)


def ffn_gradient(column, place, states):
    tokens = states[0][0].shape[0]
    count = len(states)
    anywhere = pl.BlockSpec(memory_space=pl.ANY)
    return pl.pallas_call(
        partial(ffn_gradient_kernel, column, count),
        in_specs=[pl.BlockSpec(memory_space=pltpu.SMEM)] + [anywhere] * (4 * count),
        out_specs=[pl.BlockSpec(memory_space=pltpu.VMEM), anywhere],
        out_shape=[jax.ShapeDtypeStruct((4, 4, UNIT, D), BF), jax.ShapeDtypeStruct((4, 4, UNIT, D), F32)],
        scratch_shapes=[pltpu.VMEM((count * tokens, D), BF)] * 4
        + [pltpu.VMEM((2, D, D), F32), pltpu.SemaphoreType.DMA((count, 2)), pltpu.SemaphoreType.DMA],
        compiler_params=params(),
        cost_estimate=cost(count * 5e9, 20e6),
        name=f"ffn_gradient_{column}",
    )(place, *[value for state in states for value in state])


def attention_backward_kernel(
    place_ref, x_ref, q_ref, k_ref, v_ref, o_ref, p_hbm_ref, da4_ref, da3_ref, da2_ref, da1_ref, dh1_ref, weights_hbm_ref, wo_ref,
    vg_ref, *refs
):
    (
        dx_ref, send_ref, keep_ref, dw_ref, table_ref, do_ref, sum_ref, dq_ref, dk_ref, dv_ref,
        p_ref, weights_ref, semaphore,
    ) = refs

    step = pl.program_id(0)

    def probabilities(row):
        slot = lax.rem(row, 2)
        return pltpu.make_async_copy(p_hbm_ref.at[row], p_ref.at[slot], semaphore.at[slot])

    @pl.when(pl.program_id(0) == 0)
    def _():
        dw_ref[...] = jnp.zeros_like(dw_ref)
        table_ref[...] = vg_ref[...]
        probabilities(0).start()
        pltpu.make_async_copy(weights_hbm_ref, weights_ref, semaphore.at[2]).start()

    @pl.when(step + 1 < pl.num_programs(0))
    def _():
        probabilities(step + 1).start()

    length = x_ref.shape[1]
    running = da4_ref[0].astype(F32)
    sum_ref[3] = da4_ref[0]
    for index, ref in ((2, da3_ref), (1, da2_ref), (0, da1_ref)):
        running = running + ref[0].astype(F32)
        sum_ref[index] = running.astype(BF)
    lane = lax.broadcasted_iota(jnp.int32, (length, 256), 1)
    for block in range(3):
        cols = slice(256 * block, 256 * (block + 1))
        edge = 192 * (block + 1) - 256 * block
        do_ref[:, cols] = jnp.where(
            lane < edge,
            dot(sum_ref[block], wo_ref[:, cols]),
            dot(sum_ref[block + 1], wo_ref[:, cols]),
        ).astype(BF)
        attended = o_ref[0, :, cols]
        nothing = jnp.zeros_like(attended)
        dw_ref[3, :, cols] += dot_first(
            sum_ref[block], jnp.where(lane < edge, attended, nothing)
        ) + dot_first(sum_ref[block + 1], jnp.where(lane < edge, nothing, attended))
    lane = lax.broadcasted_iota(jnp.int32, (length, 128), 1)
    probabilities(step).wait()
    slot = lax.rem(step, 2)
    dv_ref[...] = jnp.zeros_like(dv_ref)
    dk_ref[...] = jnp.zeros_like(dk_ref)
    for pair in range(PAIRS):
        cols = slice(128 * pair, 128 * (pair + 1))
        q_pair = q_ref[0, :, cols]
        k_pair = k_ref[0, :, cols]
        v_pair = v_ref[0, :, cols]
        do_pair = do_ref[:, cols]
        q_turned = q_pair.T
        do_turned = do_pair.T
        results = []
        for side in range(2):
            do_one = jnp.where((lane >= 64) == bool(side), do_pair, jnp.zeros_like(do_pair))
            heads = slice(64 * side, 64 * (side + 1))
            out = slice(128 * pair + 64 * side, 128 * pair + 64 * (side + 1))
            parts = []
            for part in range(2):
                window = slice(128 * part, 128 * part + WINDOW)
                rows = slice(HALF * part, HALF * (part + 1))
                low = p_ref[slot, 2 * pair + side, part]
                dp = dot_last(do_one[rows], v_pair[window])
                prob = low.astype(F32)
                mixed = prob * dp
                ds = (mixed - prob * jnp.sum(mixed, axis=-1, keepdims=True)).astype(BF)
                dv_ref[out, window] += dot(do_turned[heads, rows], low)
                dk_ref[out, window] += dot(q_turned[heads, rows], ds)
                parts.append(dot(ds, k_pair[window]))
            results.append(jnp.concatenate(parts, axis=0))
        dq_ref[:, cols] = (jnp.where(lane >= 64, results[1], results[0]) * SCALING).astype(BF)
    dq = dq_ref[...]

    @pl.when(step == 0)
    def _():
        all_arrived(weights_ref, semaphore.at[2])

    dk = dk_ref[...].astype(BF).T
    dv = dv_ref[...].astype(BF).T
    dx_ref[0] = (
        dh1_ref[0]
        + dot_last(dq, weights_ref[0])
        + dot_last(dk, weights_ref[1])
        + dot_last(dv, weights_ref[2])
    ).astype(BF)
    turned = x_ref[0].T
    dw_ref[0] += dot(turned, dq)
    dw_ref[1] += dot(turned, dk)
    dw_ref[2] += dot(turned, dv)
    table_ref[0:1, :] += jnp.sum(dq.astype(F32), axis=0, keepdims=True)
    table_ref[1:2, :] += jnp.sum(dv.astype(F32), axis=0, keepdims=True)

    @pl.when(pl.program_id(0) == pl.num_programs(0) - 1)
    def _():
        core = place_ref[UNITS]
        for index in range(2):
            lanes = slice(D * index, D * (index + 1))
            for plane, along, rows in blocks():
                keep_ref[plane, along, :, lanes] = dw_ref[2 * core + index, rows, :]
                send_ref[plane, along, :, lanes] = dw_ref[2 * (1 - core) + index, rows, :].astype(BF)
        lanes = slice(2 * D, 2 * D + NARROW)
        table = table_ref[...]
        nothing = jnp.zeros((UNIT - table.shape[0], NARROW), F32)
        for plane, along, rows in blocks():
            turned = pltpu.roll(table, (D - rows.start) % D, 1)[:, :NARROW]
            turned = jnp.concatenate([turned, nothing], axis=0)
            keep_ref[plane, along, :, lanes] = turned
            send_ref[plane, along, :, lanes] = turned.astype(BF)


def attention_backward(place, inputs, q, k, v, o, p, das, dh1, weights, wo, table):
    micro, length, _ = inputs.shape
    block = pl.BlockSpec((1, length, D), lambda i: (i, 0, 0))
    anywhere = pl.BlockSpec(memory_space=pl.ANY)
    lanes = 2 * D + NARROW
    return pl.pallas_call(
        attention_backward_kernel,
        grid=(micro,),
        in_specs=[pl.BlockSpec(memory_space=pltpu.SMEM)]
        + [block] * 5
        + [anywhere]
        + [block] * 5
        + [anywhere, whole((D, D)), whole((16, D))],
        out_specs=[block, whole((4, 4, UNIT, lanes)), whole((4, 4, UNIT, lanes))],
        out_shape=[
            jax.ShapeDtypeStruct((micro, length, D), BF),
            jax.ShapeDtypeStruct((4, 4, UNIT, lanes), BF),
            jax.ShapeDtypeStruct((4, 4, UNIT, lanes), F32),
        ],
        scratch_shapes=[
            pltpu.VMEM((4, D, D), F32),
            pltpu.VMEM((16, D), F32),
            pltpu.VMEM((length, D), BF),
            pltpu.VMEM((4, length, D), BF),
            pltpu.VMEM((length, D), BF),
            pltpu.VMEM((D, length), F32),
            pltpu.VMEM((D, length), F32),
            pltpu.VMEM((2, HEADS, 2, HALF, WINDOW), BF),
            pltpu.VMEM((3, D, D), BF),
            pltpu.SemaphoreType.DMA((3,)),
        ],
        compiler_params=params(),
        cost_estimate=cost(40e9, 30e6),
        name="attention_backward",
    )(place, inputs, q, k, v, o, p, *das, dh1, weights, wo, table)


AXES = ("wide", "narrow")
PLANE = (0, 4, 2, 6)
ALONG = (0, 8, 16, 24)
DEVICES = 32


def flip(value, bits):
    return lax.ppermute(value, AXES, [(device, device ^ bits) for device in range(DEVICES)])


def tie(value, *earlier):
    return lax.optimization_barrier((value, *earlier))[0] if earlier else value


class Gather:
    def __init__(self, parts, core, z):
        self.z = z
        mine = jnp.where(core == 0, parts[0], parts[1])
        theirs = flip(jnp.where(core == 0, parts[1], parts[0]), 1)
        self.unit = jnp.where(core == 0, jnp.concatenate([mine, theirs]), jnp.concatenate([theirs, mine]))

    def along(self, *earlier):
        self.unit = tie(self.unit, *earlier)
        value = [self.unit if bits == 0 else flip(self.unit, bits) for bits in ALONG]
        one, two = self.z % 2 == 1, self.z >= 2
        value = [jnp.where(one, value[index ^ 1], value[index]) for index in range(4)]
        self.near = jnp.stack([jnp.where(two, value[index ^ 2], value[index]) for index in range(4)])

    def plane(self, *earlier):
        self.near = tie(self.near, *earlier)
        self.own = [self.near if bits == 0 else flip(self.near, bits) for bits in PLANE]

    def peers(self, *earlier):
        own = [tie(piece, *earlier) for piece in self.own]
        self.peer = [flip(piece, 1) for piece in own]
        return self.own + self.peer


def gather_plain(parts):
    full = [lax.all_gather(part, AXES, axis=0, tiled=True).reshape(4, 4, UNIT, -1) for part in parts]
    return [value[:, turn] for value in full for turn in range(4)]


class Reduce:
    def __init__(self, me, send, keep, *earlier):
        self.core, self.place, self.z = me % 2, me // 2 % 4, me // 8
        self.keep = keep
        self.out = [keep]
        self.arrived = [flip(tie(send, *earlier), 1)]

    def wait(self, earlier):
        if earlier:
            self.arrived = list(lax.optimization_barrier((*self.arrived, *earlier)))[: len(self.arrived)]

    def plane(self, *earlier):
        self.wait(earlier)

        def piece(bits):
            def part(value):
                return lax.dynamic_index_in_dim(value, self.place ^ (bits // 2), 0, keepdims=False)

            return part(self.keep) + part(self.arrived[0]).astype(F32)

        self.out = [piece(bits).astype(BF) for bits in PLANE[1:]]
        self.total = piece(0)
        self.arrived = [flip(value, bits) for value, bits in zip(self.out, PLANE[1:])]

    def sum(self):
        total = self.total
        for value in self.arrived:
            total = total + value.astype(F32)
        return total

    def along(self, *earlier):
        self.wait(earlier)
        total = self.sum()

        def piece(bits):
            return lax.dynamic_index_in_dim(total, self.z ^ (bits // 8), 0, keepdims=False)

        self.out = [piece(bits).astype(BF) for bits in ALONG[1:]]
        self.total = piece(0)
        self.arrived = [flip(value, bits) for value, bits in zip(self.out, ALONG[1:])]

    def result(self, *earlier):
        self.wait(earlier)
        total = self.sum().reshape(2, OWN, -1)
        self.unit = total
        mine = lax.dynamic_index_in_dim(total, self.core, 0, keepdims=False)
        other = flip(lax.dynamic_index_in_dim(total, 1 - self.core, 0, keepdims=False), 1)
        return jnp.where(self.core == 0, mine, other), jnp.where(self.core == 0, other, mine)


def in_rows(value):
    return value.swapaxes(0, 1).reshape(D, -1)


class ReducePlain:
    def __init__(self, me, send, keep, *earlier):
        self.send, self.keep, self.out, self.arrived = send, keep, [keep], []

    def plane(self, *earlier):
        pass

    along = plane

    def result(self, *earlier):
        return [
            lax.psum_scatter(in_rows(value).astype(BF), AXES, scatter_dimension=0, tiled=True).astype(F32)
            for value in (self.keep, self.send)
        ]


def update(weights_now, momentum_now, average_now, gradient, rate):
    momentum_next = MOMENTUM * momentum_now + gradient
    weights_next = weights_now - rate * (gradient + MOMENTUM * momentum_next)
    average_next = DECAY * average_now + (1.0 - DECAY) * weights_next
    return (weights_next, momentum_next, average_next, weights_next.astype(BF))


def body(
    inputs,
    cotangent,
    doc_ids,
    attention_weights,
    attention_momentum,
    attention_average,
    feedforward_weights,
    feedforward_momentum,
    feedforward_average,
    vector_weights,
    vector_momentum,
    vector_average,
):
    micro, _, length, _ = inputs.shape
    count = lax.axis_size("wide") * lax.axis_size("narrow")
    me = lax.axis_index("wide") * lax.axis_size("narrow") + lax.axis_index("narrow")
    rows = attention_weights.shape[1]
    names = vector_weights.shape[0]
    paired = count == DEVICES
    if paired:
        core = me % 2
        offsets = [(plane ^ along) // 2 for plane in PLANE for along in ALONG]
        slots = me // 2 ^ jnp.asarray(offsets, jnp.int32)
        planes = me // 2 % 4 ^ jnp.asarray([plane // 2 for plane in PLANE], jnp.int32)
    else:
        core = jnp.zeros((), jnp.int32)
        slots = jnp.arange(UNITS, dtype=jnp.int32)
        planes = jnp.arange(4, dtype=jnp.int32)
    place = jnp.concatenate([slots, jnp.full((4,), core, jnp.int32), planes])

    attention_low = attention_weights.astype(BF)
    hidden_low = feedforward_weights.astype(BF)
    vector_low = vector_weights.astype(BF)

    def halves(value):
        return value[:, :HALF_D], value[:, HALF_D:]

    def parts_of(columns):
        return [jnp.concatenate([column[which] for column in columns], axis=1) for which in (0, 1)]

    def hidden(which):
        return tuple(hidden_low[c, :, D * which : D * (which + 1)] for c in (0, 1))

    groups = ((0, 1), (2, 3))
    parts = [
        parts_of([(attention_low[0], attention_low[2]), halves(attention_low[1])]),
        parts_of([halves(attention_low[3])] + [hidden(which) for which in groups[0]]),
        parts_of([hidden(which) for which in groups[1]]),
    ]
    inputs_rows, cotangent_rows = inputs[:, 0], cotangent[:, 0]

    def flat(value):
        return value.reshape(micro * length, D)

    def split(value):
        return value.reshape(micro, length, D)

    def forward(pieces, place):
        return attention_forward(inputs_rows, doc_ids[:, 0], place, pieces)

    if paired:
        table = jnp.pad(vector_low, ((0, OWN - names), (0, NARROW - OWN)))
        parts[0] = [jnp.concatenate([part, table], axis=1) for part in parts[0]]
        one, two, three = [Gather(part, core, me // 8) for part in parts]
        one.along()
        one.plane()
        first_pieces = one.peers()
        two.along(one.near)
        two.plane(*one.peer)
        three.along(two.near)
        q, k, v, o, p, weights, vector = forward(first_pieces, tie(place, two.near))
        second_pieces = two.peers(q, three.near)
        three.plane(q, *two.peer)
        ready = three.near
    else:
        table = lax.all_gather(vector_low, AXES, axis=1, tiled=True)
        table = table.reshape(names, UNITS, 2, OWN).transpose(1, 2, 0, 3)
        table = jnp.pad(table, ((0, 0), (0, 0), (0, OWN - names), (0, NARROW - OWN)))
        table = table.reshape(4, 4, UNIT, NARROW)
        first_pieces, second_pieces, third_pieces = [gather_plain(part) for part in parts]
        first_pieces = [
            jnp.concatenate([piece, table[:, turn % 4]], axis=2)
            for turn, piece in enumerate(first_pieces)
        ]
        q, k, v, o, p, weights, vector = forward(first_pieces, place)
        ready = place
    chunks = [(second_pieces, groups[0], HALF_D)]

    states, before, wo = {}, None, None

    def widths(quarter, *earlier):
        nonlocal before, wo
        result = ffn(
            quarter, tie(place, *earlier), flat(inputs_rows), flat(o), flat(cotangent_rows), vector, wo, chunks, before
        )
        states[quarter] = result[:5]
        before = (result[5], result[6])
        if wo is None:
            wo = result[-1]
        return result

    def gradient(which, *earlier):
        return ffn_gradient(
            which, tie(place, *earlier), [states[quarter][:4] for quarter in range(which + 1, SLICES + 1)]
        )

    reduce = Reduce if paired else ReducePlain
    widths(1, ready)
    chunks.append((three.peers(before[0]) if paired else third_pieces, groups[1], 0))
    layer_out = split(widths(4)[7])
    three = reduce(me, *gradient(3))
    widths(3, *three.out)
    three.plane(before[0])
    two = reduce(me, *gradient(2, *three.out))
    widths(2, *two.out)
    three.along(before[0])
    two.plane(*three.out)
    send, keep = gradient(1, *two.out)
    two.along(keep, *three.arrived)
    one = reduce(me, send, keep, *two.out)
    one.plane(*two.out)
    input_grad, send, keep = attention_backward(
        tie(place, *one.out), inputs_rows, q, k, v, o, p,
        [split(states[quarter][4]) for quarter in (4, 3, 2, 1)],
        split(before[0]), weights.reshape(3, D, D), wo.reshape(D, D), before[1],
    )
    one.along(keep)
    attention = reduce(me, send, keep, *one.out, *two.arrived)
    attention.plane(*one.out)
    send, keep = gradient(0, *attention.out)
    attention.along(keep, *one.arrived)
    zero = reduce(me, send, keep, *attention.out)
    zero.plane(*attention.out)
    three_sum, two_sum, one_sum = [value.result(*zero.out) for value in (three, two, one)]
    attention_sum = attention.result(*zero.out)
    zero.along(*zero.out)
    sums = [zero.result(), one_sum, two_sum, three_sum]

    attention_gradient = jnp.stack(
        [attention_sum[index // 2][:, D * (index % 2) : D * (index % 2 + 1)] for index in range(4)]
    )
    feedforward_gradient = jnp.stack([jnp.concatenate([value[c] for value in sums], axis=1) for c in (0, 1)])
    if paired:
        table = attention.unit[0, :names, 2 * D : 2 * D + UNIT]
        vector_gradient = lax.dynamic_slice_in_dim(table, OWN * core, OWN, 1)
    else:
        table = in_rows(attention.keep)[:, 2 * D : 2 * D + UNIT].reshape(UNITS, UNIT, UNIT)[:, :names]
        table = table.transpose(1, 0, 2).reshape(names, D)
        vector_gradient = lax.psum_scatter(table, AXES, scatter_dimension=1, tiled=True)

    rate = 0.05 / math.sqrt(micro * length * count)
    return (
        layer_out[:, None],
        input_grad[:, None],
        *update(attention_weights, attention_momentum, attention_average, attention_gradient, rate),
        *update(feedforward_weights, feedforward_momentum, feedforward_average, feedforward_gradient, rate),
        *update(vector_weights, vector_momentum, vector_average, vector_gradient, rate),
    )


def solution(mesh):
    row = P(None, AXES, None, None)
    matrix = P(None, AXES, None)
    table = P(None, AXES)
    in_specs = (row, row, matrix) + (matrix,) * 6 + (table,) * 3
    out_specs = (row, row) + (matrix,) * 8 + (table,) * 4
    return jax.shard_map(body, mesh=mesh, in_specs=in_specs, out_specs=out_specs, check_vma=False)
```

```python
from functools import partial
import math

import jax
import jax.numpy as jnp
from jax import lax
from jax.experimental import pallas as pl
from jax.experimental.pallas import tpu as pltpu
from jax.sharding import PartitionSpec as P

D = 768
HEADS = 12
HEAD_DIM = 64
FF = 3072
SLICES = FF // D
PAIRS = HEADS // 2
HALF = 256
WINDOW = 384

EPSILON = 1e-12
SCALING = 0.125
MASKED = -1000000000.0
MOMENTUM = 0.5
DECAY = 0.5
BF = jnp.bfloat16
F32 = jnp.float32

TILE = 256
TALL = 256
VMEM_LIMIT = 60 * 1024 * 1024


def dot(left, right):
    return lax.dot_general(left, right, (((1,), (0,)), ((), ())), preferred_element_type=F32)


def dot_last(left, right):
    return lax.dot_general(left, right, (((1,), (1,)), ((), ())), preferred_element_type=F32)


def dot_first(left, right):
    return lax.dot_general(left, right, (((0,), (0,)), ((), ())), preferred_element_type=F32)


def whole(shape):
    zeros = (0,) * len(shape)
    return pl.BlockSpec(shape, lambda *_: zeros, pipeline_mode=pl.Buffered(1))


def params():
    return pltpu.CompilerParams(vmem_limit_bytes=VMEM_LIMIT)


PIECES = 8
UNITS = 16
UNIT = D // UNITS
OWN = UNIT // 2
HALF_D = D // 2
NARROW = 128


def load(pieces, place_ref, moves, semaphore):
    for own in (True, False):
        for turn in range(4):
            piece = pieces[turn if own else 4 + turn]
            for lane, lanes, target in moves:
                pltpu.make_async_copy(
                    piece.at[:, :, lane : lane + lanes],
                    target(own).at[:, place_ref[UNITS + 4 + turn]],
                    semaphore,
                ).start()


def all_arrived(ref, semaphore):
    pltpu.make_async_copy(ref, ref, semaphore).wait()


def cost(flops, size):
    return pl.CostEstimate(flops=int(flops), bytes_accessed=int(size), transcendentals=0)


def attention_forward_kernel(place_ref, x_ref, column_ref, row_ref, *refs):
    pieces, refs = refs[:PIECES], refs[PIECES:]
    q_ref, k_ref, v_ref, o_ref, p_ref, weights_ref, vector_ref, table_ref, semaphore = refs


    @pl.when(pl.program_id(0) == 0)
    def _():
        core = place_ref[UNITS]

        def half(own):
            which = core if own else 1 - core
            return weights_ref.at[1, :, :, :, pl.ds(pl.multiple_of(HALF_D * which, NARROW), HALF_D)]

        load(
            pieces,
            place_ref,
            (
                (0, D, lambda own: weights_ref.at[2 * (core if own else 1 - core)]),
                (D, HALF_D, half),
            ),
            semaphore.at[0],
        )
        for turn in range(4):
            pltpu.make_async_copy(
                pieces[turn].at[:, :, D + HALF_D : D + HALF_D + NARROW],
                table_ref.at[pl.ds(4 * turn, 4)],
                semaphore.at[1],
            ).start()
        all_arrived(table_ref, semaphore.at[1])
        vector = jnp.zeros((16, D), F32)
        for slot in range(UNITS):
            unit = table_ref[slot].astype(F32)
            for one in range(2):
                part = unit[OWN * one : OWN * one + 16]
                wide = jnp.concatenate([part, jnp.zeros((16, D - NARROW), F32)], axis=1)
                unit_number = 4 * (slot % 4) + place_ref[UNITS + 4 + slot // 4]
                vector = vector + pltpu.roll(wide, UNIT * unit_number + OWN * one, 1)
        vector_ref[...] = vector
        all_arrived(weights_ref, semaphore.at[0])

    rows = x_ref[0]
    queries = (dot(rows, weights_ref[0].reshape(D, D)) + vector_ref[0:1, :]).astype(BF)
    q_ref[0] = queries * jnp.asarray(SCALING, BF)
    k_ref[0] = dot(rows, weights_ref[1].reshape(D, D)).astype(BF)
    v_ref[0] = (dot(rows, weights_ref[2].reshape(D, D)) + vector_ref[1:2, :]).astype(BF)
    length = rows.shape[0]
    lane = lax.broadcasted_iota(jnp.int32, (length, 128), 1)
    masks = [
        column_ref[0, HALF * part : HALF * (part + 1), :]
        == row_ref[0, :, 128 * part : 128 * part + WINDOW]
        for part in range(2)
    ]
    items = [(side, part) for side in range(2) for part in range(2)]

    def scores_of(pair):
        cols = slice(128 * pair, 128 * (pair + 1))
        q_pair = q_ref[0, :, cols]
        k_pair = k_ref[0, :, cols]
        found = []
        for side, part in items:
            q_one = jnp.where((lane >= 64) == bool(side), q_pair, jnp.zeros_like(q_pair))
            window = slice(128 * part, 128 * part + WINDOW)
            scores = dot_last(q_one[HALF * part : HALF * (part + 1)], k_pair[window])
            found.append(jnp.where(masks[part], scores, MASKED))
        return found

    def finish(pair, found):
        cols = slice(128 * pair, 128 * (pair + 1))
        v_pair = v_ref[0, :, cols]
        lows = []
        for (side, part), scores in zip(items, found):
            peak = jnp.max(scores, axis=-1, keepdims=True)
            exponent = jnp.exp(scores - peak)
            total = jnp.sum(exponent, axis=-1, keepdims=True)
            low = (exponent * (1.0 / total)).astype(BF)
            p_ref[0, 2 * pair + side, part] = low
            lows.append(low)
        parts = [dot(low, v_pair[128 * part : 128 * part + WINDOW]) for (side, part), low in zip(items, lows)]
        results = [jnp.concatenate(parts[:2], axis=0), jnp.concatenate(parts[2:], axis=0)]
        o_ref[0, :, cols] = jnp.where(lane >= 64, results[1], results[0]).astype(BF)

    for pair in range(PAIRS):
        finish(pair, scores_of(pair))


def attention_forward(inputs, documents, place, pieces):
    micro, length, _ = inputs.shape
    block = pl.BlockSpec((1, length, D), lambda i: (i, 0, 0))
    shape = jax.ShapeDtypeStruct((micro, length, D), BF)
    return pl.pallas_call(
        attention_forward_kernel,
        grid=(micro,),
        in_specs=[
            pl.BlockSpec(memory_space=pltpu.SMEM),
            block,
            pl.BlockSpec((1, length, 1), lambda i: (i, 0, 0)),
            pl.BlockSpec((1, 1, length), lambda i: (i, 0, 0)),
        ]
        + [pl.BlockSpec(memory_space=pl.ANY)] * PIECES,
        out_specs=[block] * 4
        + [
            pl.BlockSpec((1, HEADS, 2, HALF, WINDOW), lambda i: (i, 0, 0, 0, 0)),
            whole((3, 4, 4, UNIT, D)),
            whole((16, D)),
        ],
        out_shape=[shape] * 4
        + [
            jax.ShapeDtypeStruct((micro, HEADS, 2, HALF, WINDOW), BF),
            jax.ShapeDtypeStruct((3, 4, 4, UNIT, D), BF),
            jax.ShapeDtypeStruct((16, D), F32),
        ],
        scratch_shapes=[pltpu.VMEM((UNITS, UNIT, NARROW), BF), pltpu.SemaphoreType.DMA((2,))],
        cost_estimate=cost(18e9, 20e6),
        compiler_params=params(),
        name="attention_forward",
    )(place, inputs, documents[:, :, None], documents[:, None, :], *pieces)


def gelu_terms(pre):
    below = 0.5 + 0.5 * lax.erf(pre * math.sqrt(0.5))
    bell = jnp.exp2(pre * pre * (-0.5 * math.log2(math.e)))
    return pre * below, below + (pre * (1.0 / math.sqrt(2.0 * math.pi))) * bell


def mean_of(value):
    return jnp.sum(value, axis=-1, keepdims=True) * (1.0 / D)


def norm_forward(summed):
    centered = summed - mean_of(summed)
    inverse = lax.rsqrt(mean_of(centered * centered) + EPSILON)
    return centered * inverse, inverse


def norm_backward(scaled, normed, inverse):
    return inverse * (scaled - mean_of(scaled) - normed * mean_of(scaled * normed))


def ffn_kernel(quarter, first, layout, *refs):
    refs = list(refs)
    place_ref, x_ref, o_ref, cotangent_ref, vector_ref = refs[:5]
    refs = refs[5:]
    if not first:
        wo_ref, refs = refs[0], refs[1:]
    chunks, refs = refs[: PIECES * len(layout)], refs[PIECES * len(layout) :]
    if not first:
        before_ref, vg_before_ref = refs[:2]
        refs = refs[2:]
    x1_ref, dm_ref, g_ref, du_ref, da_ref, dh1_ref, vg_ref = refs[:7]
    refs = refs[7:]
    if quarter == SLICES:
        out_ref = refs[0]
        refs = refs[1:]
    if first:
        wo_ref, refs = refs[0], refs[1:]
    slope_ref, total_ref, weights_ref, semaphore = refs

    @pl.when(pl.program_id(0) == 0)
    def _():
        core = place_ref[UNITS]

        def half(own):
            which = core if own else 1 - core
            return wo_ref.at[:, :, :, pl.ds(pl.multiple_of(HALF_D * which, NARROW), HALF_D)]

        for index, (slices, lane) in enumerate(layout):
            pieces = chunks[PIECES * index : PIECES * (index + 1)]
            if index == 0 and first:
                load(pieces, place_ref, ((0, HALF_D, half),), semaphore.at[SLICES])
            count = min(len(slices), quarter - slices[0])
            lanes = slice(D * slices[0], D * (slices[0] + count))
            load(
                pieces,
                place_ref,
                ((lane, D * count, lambda own, lanes=lanes: weights_ref.at[core if own else 1 - core, :, :, :, lanes]),),
                semaphore.at[index],
            )
        if first:
            vg_ref[...] = jnp.zeros_like(vg_ref)
        else:
            vg_ref[...] = vg_before_ref[...]

    def arrived(index):
        @pl.when(pl.program_id(0) == 0)
        def _():
            slices = layout[index][0]
            count = min(len(slices), quarter - slices[0])
            ref = weights_ref.at[:, :, :, :, D * slices[0] : D * (slices[0] + count)]
            all_arrived(ref, semaphore.at[index])

    def vector(index):
        return vector_ref[index : index + 1, :]

    if first:

        @pl.when(pl.program_id(0) == 0)
        def _():
            all_arrived(wo_ref, semaphore.at[SLICES])

    def add_row(index, value, lanes=slice(0, D)):
        vg_ref[index : index + 1, lanes] += jnp.sum(value, axis=0, keepdims=True)

    width = 192 * quarter
    padded = -(-width // 128) * 128
    length = x_ref.shape[0]
    tops = range(0, length, TALL)
    ones, centers = {}, {}
    wo = wo_ref[...].reshape(D, D)[:, :padded]
    for top in tops:
        rows = slice(top, top + TALL)
        attended = o_ref[rows, :padded]
        if padded != width:
            lane = lax.broadcasted_iota(jnp.int32, attended.shape, 1)
            attended = jnp.where(lane < width, attended, jnp.zeros_like(attended))
        branch = dot_last(attended, wo) + vector(2)
        ones[top] = norm_forward(x_ref[rows, :].astype(F32) + branch)
        first_norm = ones[top][0] * vector(8) + vector(9)
        x1_ref[rows, :] = first_norm.astype(BF)
        total_ref[rows, :] = first_norm + vector(7)
    for index in range(quarter):
        for number, (slices, _) in enumerate(layout):
            if slices[0] == index:
                arrived(number)
        for top in range(0, length, TILE):
            for column in range(D * index, D * (index + 1), TILE):
                rows, cols = slice(top, top + TILE), slice(column, column + TILE)
                lanes = slice(column % D, column % D + TILE)
                matrix = weights_ref[0, :, :, :, cols].reshape(D, TILE)
                pre = dot(x1_ref[rows, :], matrix) + vector_ref[3 + index : 4 + index, lanes]
                value, slope = gelu_terms(pre)
                g_ref[rows, cols] = value.astype(BF)
                slope_ref[rows, cols] = slope
    down = weights_ref[1].reshape(D, D * quarter)
    for top in tops:
        rows = slice(top, top + TALL)
        normed, inverse = norm_forward(total_ref[rows, :] + dot_last(g_ref[rows, :], down))
        upstream = cotangent_ref[rows, :].astype(F32)
        if quarter == SLICES:
            out_ref[rows, :] = (normed * vector(10) + vector(11)).astype(BF)
            add_row(11, upstream * float(SLICES))
        add_row(10, upstream * normed)
        grad = norm_backward(upstream * vector(10), normed, inverse)
        low = grad.astype(BF)
        dm_ref[rows, :] = low
        add_row(7, low.astype(F32))
        total_ref[rows, :] = grad
    for index in range(quarter):
        for top in range(0, length, TILE):
            for column in range(D * index, D * (index + 1), TILE):
                rows, cols = slice(top, top + TILE), slice(column, column + TILE)
                lanes = slice(column % D, column % D + TILE)
                matrix = weights_ref[1, :, :, :, cols].reshape(D, TILE)
                pre = (dot(dm_ref[rows, :], matrix) * slope_ref[rows, cols]).astype(BF)
                du_ref[rows, cols] = pre
                add_row(3 + index, pre.astype(F32), lanes)
    up = weights_ref[0].reshape(D, D * quarter)
    for top in tops:
        rows = slice(top, top + TALL)
        normed, inverse = ones[top]
        grad = total_ref[rows, :] + dot_last(du_ref[rows, :], up)
        add_row(9, grad)
        add_row(8, grad * normed)
        grad = norm_backward(grad * vector(8), normed, inverse)
        low = grad.astype(BF)
        da_ref[rows, :] = low
        add_row(2, low.astype(F32))
        if first:
            dh1_ref[rows, :] = grad
        else:
            dh1_ref[rows, :] = before_ref[rows, :] + grad


def ffn(quarter, place, inputs, attended, cotangent, vector, wo, chunks, before, block=512):
    tokens = inputs.shape[0]
    hidden = D * quarter
    rows = pl.BlockSpec((block, D), lambda i: (i, 0))
    wide = pl.BlockSpec((block, hidden), lambda i: (i, 0))
    first = wo is None
    low = jax.ShapeDtypeStruct((tokens, D), BF)
    low_wide = jax.ShapeDtypeStruct((tokens, hidden), BF)
    anywhere = pl.BlockSpec(memory_space=pl.ANY)
    chunks = [chunk for chunk in chunks if min(chunk[1]) < quarter]
    in_specs = [pl.BlockSpec(memory_space=pltpu.SMEM), rows, rows, rows, whole((16, D))]
    args = [place, inputs, attended, cotangent, vector]
    if not first:
        in_specs.append(whole((4, 4, UNIT, D)))
        args.append(wo)
    for chunk in chunks:
        in_specs += [anywhere] * PIECES
        args += list(chunk[0])
    if not first:
        in_specs += [rows, whole((16, D))]
        args += list(before)
    out_specs = [rows, rows, wide, wide, rows, rows, whole((16, D))]
    out_shape = [
        low,
        low,
        low_wide,
        low_wide,
        low,
        jax.ShapeDtypeStruct((tokens, D), F32),
        jax.ShapeDtypeStruct((16, D), F32),
    ]
    if quarter == SLICES:
        out_specs.append(rows)
        out_shape.append(low)
    if first:
        out_specs.append(whole((4, 4, UNIT, D)))
        out_shape.append(jax.ShapeDtypeStruct((4, 4, UNIT, D), BF))
    layout = [(chunk[1], chunk[2]) for chunk in chunks]
    return pl.pallas_call(
        partial(ffn_kernel, quarter, first, layout),
        grid=(tokens // block,),
        in_specs=in_specs,
        out_specs=out_specs,
        out_shape=out_shape,
        scratch_shapes=[
            pltpu.VMEM((block, hidden), F32),
            pltpu.VMEM((block, D), F32),
            pltpu.VMEM((2, 4, 4, UNIT, hidden), BF),
            pltpu.SemaphoreType.DMA((SLICES + 1,)),
        ],
        compiler_params=params(),
        cost_estimate=cost(8e9 + quarter * 9e9, 20e6),
        name=f"ffn_{quarter}",
    )(*args)


def blocks():
    for plane in range(4):
        for along in range(4):
            start = UNIT * (4 * along + plane)
            yield plane, along, slice(start, start + UNIT)


def ffn_gradient_kernel(column, count, place_ref, *refs):
    inputs, refs = refs[: 4 * count], refs[4 * count :]
    send_ref, keep_ref, x1_ref, du_ref, dm_ref, g_ref, total_ref, semaphore, keep_semaphore = refs
    size = inputs[0].shape[0]
    cols = slice(D * column, D * (column + 1))

    def copies(index, turn):
        rows = slice(size * index, size * (index + 1))
        low, grad, value, pre = inputs[4 * index : 4 * index + 4]
        pairs = (((low, x1_ref), (pre.at[:, cols], du_ref)), ((grad, dm_ref), (value.at[:, cols], g_ref)))[turn]
        return [pltpu.make_async_copy(source, target.at[rows], semaphore.at[index, turn]) for source, target in pairs]

    def start(index, turn):
        for copy in copies(index, turn):
            copy.start()

    order = [(index, turn) for index in range(count) for turn in range(2)]
    for item in order[:1]:
        start(*item)
    for number, (index, turn) in enumerate(order):
        for copy in copies(index, turn):
            copy.wait()
        for item in order[2 * number + 1 : 2 * number + 3]:
            start(*item)
        rows = slice(size * index, size * (index + 1))
        left, right = ((x1_ref, du_ref), (dm_ref, g_ref))[turn]
        product = dot_first(left[rows, :], right[rows, :])
        if index == 0:
            total_ref[turn] = product
        else:
            total_ref[turn] += product
    core = place_ref[UNITS]
    for plane, along, rows in blocks():
        pltpu.make_async_copy(total_ref.at[core, rows], keep_ref.at[plane, along], keep_semaphore).start()
    for plane, along, rows in blocks():
        send_ref[plane, along] = total_ref[1 - core, rows, :].astype(BF)
    all_arrived(keep_ref, keep_semaphore)


def ffn_gradient(column, place, states):
    tokens = states[0][0].shape[0]
    count = len(states)
    anywhere = pl.BlockSpec(memory_space=pl.ANY)
    return pl.pallas_call(
        partial(ffn_gradient_kernel, column, count),
        in_specs=[pl.BlockSpec(memory_space=pltpu.SMEM)] + [anywhere] * (4 * count),
        out_specs=[pl.BlockSpec(memory_space=pltpu.VMEM), anywhere],
        out_shape=[jax.ShapeDtypeStruct((4, 4, UNIT, D), BF), jax.ShapeDtypeStruct((4, 4, UNIT, D), F32)],
        scratch_shapes=[pltpu.VMEM((count * tokens, D), BF)] * 4
        + [pltpu.VMEM((2, D, D), F32), pltpu.SemaphoreType.DMA((count, 2)), pltpu.SemaphoreType.DMA],
        compiler_params=params(),
        cost_estimate=cost(count * 5e9, 20e6),
        name=f"ffn_gradient_{column}",
    )(place, *[value for state in states for value in state])


def attention_backward_kernel(
    place_ref, x_ref, q_ref, k_ref, v_ref, o_ref, p_hbm_ref, da4_ref, da3_ref, da2_ref, da1_ref, dh1_ref, weights_hbm_ref, wo_ref,
    vg_ref, *refs
):
    (
        dx_ref, send_ref, keep_ref, dw_ref, table_ref, do_ref, sum_ref, dq_ref, dk_ref, dv_ref,
        p_ref, weights_ref, semaphore,
    ) = refs

    step = pl.program_id(0)

    def probabilities(row):
        slot = lax.rem(row, 2)
        return pltpu.make_async_copy(p_hbm_ref.at[row], p_ref.at[slot], semaphore.at[slot])

    @pl.when(pl.program_id(0) == 0)
    def _():
        dw_ref[...] = jnp.zeros_like(dw_ref)
        table_ref[...] = vg_ref[...]
        probabilities(0).start()
        pltpu.make_async_copy(weights_hbm_ref, weights_ref, semaphore.at[2]).start()

    @pl.when(step + 1 < pl.num_programs(0))
    def _():
        probabilities(step + 1).start()

    length = x_ref.shape[1]
    running = da4_ref[0].astype(F32)
    sum_ref[3] = da4_ref[0]
    for index, ref in ((2, da3_ref), (1, da2_ref), (0, da1_ref)):
        running = running + ref[0].astype(F32)
        sum_ref[index] = running.astype(BF)
    lane = lax.broadcasted_iota(jnp.int32, (length, 256), 1)
    for block in range(3):
        cols = slice(256 * block, 256 * (block + 1))
        edge = 192 * (block + 1) - 256 * block
        do_ref[:, cols] = jnp.where(
            lane < edge,
            dot(sum_ref[block], wo_ref[:, cols]),
            dot(sum_ref[block + 1], wo_ref[:, cols]),
        ).astype(BF)
        attended = o_ref[0, :, cols]
        nothing = jnp.zeros_like(attended)
        dw_ref[3, :, cols] += dot_first(
            sum_ref[block], jnp.where(lane < edge, attended, nothing)
        ) + dot_first(sum_ref[block + 1], jnp.where(lane < edge, nothing, attended))
    lane = lax.broadcasted_iota(jnp.int32, (length, 128), 1)
    probabilities(step).wait()
    slot = lax.rem(step, 2)
    dv_ref[...] = jnp.zeros_like(dv_ref)
    dk_ref[...] = jnp.zeros_like(dk_ref)
    for pair in range(PAIRS):
        cols = slice(128 * pair, 128 * (pair + 1))
        q_pair = q_ref[0, :, cols]
        k_pair = k_ref[0, :, cols]
        v_pair = v_ref[0, :, cols]
        do_pair = do_ref[:, cols]
        q_turned = q_pair.T
        do_turned = do_pair.T
        items = [(side, part) for side in range(2) for part in range(2)]
        windows = [slice(128 * part, 128 * part + WINDOW) for part in range(2)]
        halves = [slice(HALF * part, HALF * (part + 1)) for part in range(2)]
        products = []
        for side, part in items:
            do_one = jnp.where((lane >= 64) == bool(side), do_pair, jnp.zeros_like(do_pair))
            products.append(dot_last(do_one[halves[part]], v_pair[windows[part]]))
        lows = []
        for (side, part), dp in zip(items, products):
            prob = p_ref[slot, 2 * pair + side, part].astype(F32)
            mixed = prob * dp
            lows.append((mixed - prob * jnp.sum(mixed, axis=-1, keepdims=True)).astype(BF))
        parts = []
        for (side, part), ds in zip(items, lows):
            heads = slice(64 * side, 64 * (side + 1))
            out = slice(128 * pair + 64 * side, 128 * pair + 64 * (side + 1))
            window, rows = windows[part], halves[part]
            dv_ref[out, window] += dot(do_turned[heads, rows], p_ref[slot, 2 * pair + side, part])
            dk_ref[out, window] += dot(q_turned[heads, rows], ds)
            parts.append(dot(ds, k_pair[window]))
        results = [jnp.concatenate(parts[:2], axis=0), jnp.concatenate(parts[2:], axis=0)]
        dq_ref[:, cols] = (jnp.where(lane >= 64, results[1], results[0]) * SCALING).astype(BF)
    dq = dq_ref[...]

    @pl.when(step == 0)
    def _():
        all_arrived(weights_ref, semaphore.at[2])

    dk = dk_ref[...].astype(BF).T
    dv = dv_ref[...].astype(BF).T
    dx_ref[0] = (
        dh1_ref[0]
        + dot_last(dq, weights_ref[0])
        + dot_last(dk, weights_ref[1])
        + dot_last(dv, weights_ref[2])
    ).astype(BF)
    turned = x_ref[0].T
    dw_ref[0] += dot(turned, dq)
    dw_ref[1] += dot(turned, dk)
    dw_ref[2] += dot(turned, dv)
    table_ref[0:1, :] += jnp.sum(dq.astype(F32), axis=0, keepdims=True)
    table_ref[1:2, :] += jnp.sum(dv.astype(F32), axis=0, keepdims=True)

    @pl.when(pl.program_id(0) == pl.num_programs(0) - 1)
    def _():
        core = place_ref[UNITS]
        for index in range(2):
            lanes = slice(D * index, D * (index + 1))
            for plane, along, rows in blocks():
                keep_ref[plane, along, :, lanes] = dw_ref[2 * core + index, rows, :]
                send_ref[plane, along, :, lanes] = dw_ref[2 * (1 - core) + index, rows, :].astype(BF)
        lanes = slice(2 * D, 2 * D + NARROW)
        table = table_ref[...]
        nothing = jnp.zeros((UNIT - table.shape[0], NARROW), F32)
        for plane, along, rows in blocks():
            turned = pltpu.roll(table, (D - rows.start) % D, 1)[:, :NARROW]
            turned = jnp.concatenate([turned, nothing], axis=0)
            keep_ref[plane, along, :, lanes] = turned
            send_ref[plane, along, :, lanes] = turned.astype(BF)


def attention_backward(place, inputs, q, k, v, o, p, das, dh1, weights, wo, table):
    micro, length, _ = inputs.shape
    block = pl.BlockSpec((1, length, D), lambda i: (i, 0, 0))
    anywhere = pl.BlockSpec(memory_space=pl.ANY)
    lanes = 2 * D + NARROW
    return pl.pallas_call(
        attention_backward_kernel,
        grid=(micro,),
        in_specs=[pl.BlockSpec(memory_space=pltpu.SMEM)]
        + [block] * 5
        + [anywhere]
        + [block] * 5
        + [anywhere, whole((D, D)), whole((16, D))],
        out_specs=[block, whole((4, 4, UNIT, lanes)), whole((4, 4, UNIT, lanes))],
        out_shape=[
            jax.ShapeDtypeStruct((micro, length, D), BF),
            jax.ShapeDtypeStruct((4, 4, UNIT, lanes), BF),
            jax.ShapeDtypeStruct((4, 4, UNIT, lanes), F32),
        ],
        scratch_shapes=[
            pltpu.VMEM((4, D, D), F32),
            pltpu.VMEM((16, D), F32),
            pltpu.VMEM((length, D), BF),
            pltpu.VMEM((4, length, D), BF),
            pltpu.VMEM((length, D), BF),
            pltpu.VMEM((D, length), F32),
            pltpu.VMEM((D, length), F32),
            pltpu.VMEM((2, HEADS, 2, HALF, WINDOW), BF),
            pltpu.VMEM((3, D, D), BF),
            pltpu.SemaphoreType.DMA((3,)),
        ],
        compiler_params=params(),
        cost_estimate=cost(40e9, 30e6),
        name="attention_backward",
    )(place, inputs, q, k, v, o, p, *das, dh1, weights, wo, table)


AXES = ("wide", "narrow")
PLANE = (0, 4, 2, 6)
ALONG = (0, 8, 16, 24)
DEVICES = 32


def flip(value, bits):
    return lax.ppermute(value, AXES, [(device, device ^ bits) for device in range(DEVICES)])


def tie(value, *earlier):
    return lax.optimization_barrier((value, *earlier))[0] if earlier else value


class Gather:
    def __init__(self, parts, core, z):
        self.z = z
        mine = jnp.where(core == 0, parts[0], parts[1])
        theirs = flip(jnp.where(core == 0, parts[1], parts[0]), 1)
        self.unit = jnp.where(core == 0, jnp.concatenate([mine, theirs]), jnp.concatenate([theirs, mine]))

    def along(self, *earlier):
        self.unit = tie(self.unit, *earlier)
        value = [self.unit if bits == 0 else flip(self.unit, bits) for bits in ALONG]
        one, two = self.z % 2 == 1, self.z >= 2
        value = [jnp.where(one, value[index ^ 1], value[index]) for index in range(4)]
        self.near = jnp.stack([jnp.where(two, value[index ^ 2], value[index]) for index in range(4)])

    def plane(self, *earlier):
        self.near = tie(self.near, *earlier)
        self.own = [self.near if bits == 0 else flip(self.near, bits) for bits in PLANE]

    def peers(self, *earlier):
        own = [tie(piece, *earlier) for piece in self.own]
        self.peer = [flip(piece, 1) for piece in own]
        return self.own + self.peer


def gather_plain(parts):
    full = [lax.all_gather(part, AXES, axis=0, tiled=True).reshape(4, 4, UNIT, -1) for part in parts]
    return [value[:, turn] for value in full for turn in range(4)]


class Reduce:
    def __init__(self, me, send, keep, *earlier):
        self.core, self.place, self.z = me % 2, me // 2 % 4, me // 8
        self.keep = keep
        self.out = [keep]
        self.arrived = [flip(tie(send, *earlier), 1)]

    def wait(self, earlier):
        if earlier:
            self.arrived = list(lax.optimization_barrier((*self.arrived, *earlier)))[: len(self.arrived)]

    def plane(self, *earlier):
        self.wait(earlier)

        def piece(bits):
            def part(value):
                return lax.dynamic_index_in_dim(value, self.place ^ (bits // 2), 0, keepdims=False)

            return part(self.keep) + part(self.arrived[0]).astype(F32)

        self.out = [piece(bits).astype(BF) for bits in PLANE[1:]]
        self.total = piece(0)
        self.arrived = [flip(value, bits) for value, bits in zip(self.out, PLANE[1:])]

    def sum(self):
        total = self.total
        for value in self.arrived:
            total = total + value.astype(F32)
        return total

    def along(self, *earlier):
        self.wait(earlier)
        total = self.sum()

        def piece(bits):
            return lax.dynamic_index_in_dim(total, self.z ^ (bits // 8), 0, keepdims=False)

        self.out = [piece(bits).astype(BF) for bits in ALONG[1:]]
        self.total = piece(0)
        self.arrived = [flip(value, bits) for value, bits in zip(self.out, ALONG[1:])]

    def result(self, *earlier):
        self.wait(earlier)
        total = self.sum().reshape(2, OWN, -1)
        self.unit = total
        mine = lax.dynamic_index_in_dim(total, self.core, 0, keepdims=False)
        other = flip(lax.dynamic_index_in_dim(total, 1 - self.core, 0, keepdims=False), 1)
        return jnp.where(self.core == 0, mine, other), jnp.where(self.core == 0, other, mine)


def in_rows(value):
    return value.swapaxes(0, 1).reshape(D, -1)


class ReducePlain:
    def __init__(self, me, send, keep, *earlier):
        self.send, self.keep, self.out, self.arrived = send, keep, [keep], []

    def plane(self, *earlier):
        pass

    along = plane

    def result(self, *earlier):
        return [
            lax.psum_scatter(in_rows(value).astype(BF), AXES, scatter_dimension=0, tiled=True).astype(F32)
            for value in (self.keep, self.send)
        ]


def update(weights_now, momentum_now, average_now, gradient, rate):
    momentum_next = MOMENTUM * momentum_now + gradient
    weights_next = weights_now - rate * (gradient + MOMENTUM * momentum_next)
    average_next = DECAY * average_now + (1.0 - DECAY) * weights_next
    return (weights_next, momentum_next, average_next, weights_next.astype(BF))


def body(
    inputs,
    cotangent,
    doc_ids,
    attention_weights,
    attention_momentum,
    attention_average,
    feedforward_weights,
    feedforward_momentum,
    feedforward_average,
    vector_weights,
    vector_momentum,
    vector_average,
):
    micro, _, length, _ = inputs.shape
    count = lax.axis_size("wide") * lax.axis_size("narrow")
    me = lax.axis_index("wide") * lax.axis_size("narrow") + lax.axis_index("narrow")
    rows = attention_weights.shape[1]
    names = vector_weights.shape[0]
    paired = count == DEVICES
    if paired:
        core = me % 2
        offsets = [(plane ^ along) // 2 for plane in PLANE for along in ALONG]
        slots = me // 2 ^ jnp.asarray(offsets, jnp.int32)
        planes = me // 2 % 4 ^ jnp.asarray([plane // 2 for plane in PLANE], jnp.int32)
    else:
        core = jnp.zeros((), jnp.int32)
        slots = jnp.arange(UNITS, dtype=jnp.int32)
        planes = jnp.arange(4, dtype=jnp.int32)
    place = jnp.concatenate([slots, jnp.full((4,), core, jnp.int32), planes])

    attention_low = attention_weights.astype(BF)
    hidden_low = feedforward_weights.astype(BF)
    vector_low = vector_weights.astype(BF)

    def halves(value):
        return value[:, :HALF_D], value[:, HALF_D:]

    def parts_of(columns):
        return [jnp.concatenate([column[which] for column in columns], axis=1) for which in (0, 1)]

    def hidden(which):
        return tuple(hidden_low[c, :, D * which : D * (which + 1)] for c in (0, 1))

    groups = ((0, 1), (2, 3))
    parts = [
        parts_of([(attention_low[0], attention_low[2]), halves(attention_low[1])]),
        parts_of([halves(attention_low[3])] + [hidden(which) for which in groups[0]]),
        parts_of([hidden(which) for which in groups[1]]),
    ]
    inputs_rows, cotangent_rows = inputs[:, 0], cotangent[:, 0]

    def flat(value):
        return value.reshape(micro * length, D)

    def split(value):
        return value.reshape(micro, length, D)

    def forward(pieces, place):
        return attention_forward(inputs_rows, doc_ids[:, 0], place, pieces)

    if paired:
        table = jnp.pad(vector_low, ((0, OWN - names), (0, NARROW - OWN)))
        parts[0] = [jnp.concatenate([part, table], axis=1) for part in parts[0]]
        one, two, three = [Gather(part, core, me // 8) for part in parts]
        one.along()
        one.plane()
        first_pieces = one.peers()
        two.along(one.near)
        two.plane(*one.peer)
        three.along(two.near)
        q, k, v, o, p, weights, vector = forward(first_pieces, tie(place, two.near))
        second_pieces = two.peers(q, three.near)
        three.plane(q, *two.peer)
        ready = three.near
    else:
        table = lax.all_gather(vector_low, AXES, axis=1, tiled=True)
        table = table.reshape(names, UNITS, 2, OWN).transpose(1, 2, 0, 3)
        table = jnp.pad(table, ((0, 0), (0, 0), (0, OWN - names), (0, NARROW - OWN)))
        table = table.reshape(4, 4, UNIT, NARROW)
        first_pieces, second_pieces, third_pieces = [gather_plain(part) for part in parts]
        first_pieces = [
            jnp.concatenate([piece, table[:, turn % 4]], axis=2)
            for turn, piece in enumerate(first_pieces)
        ]
        q, k, v, o, p, weights, vector = forward(first_pieces, place)
        ready = place
    chunks = [(second_pieces, groups[0], HALF_D)]

    states, before, wo = {}, None, None

    def widths(quarter, *earlier):
        nonlocal before, wo
        result = ffn(
            quarter, tie(place, *earlier), flat(inputs_rows), flat(o), flat(cotangent_rows), vector, wo, chunks, before
        )
        states[quarter] = result[:5]
        before = (result[5], result[6])
        if wo is None:
            wo = result[-1]
        return result

    def gradient(which, *earlier):
        return ffn_gradient(
            which, tie(place, *earlier), [states[quarter][:4] for quarter in range(which + 1, SLICES + 1)]
        )

    reduce = Reduce if paired else ReducePlain
    widths(1, ready)
    chunks.append((three.peers(before[0]) if paired else third_pieces, groups[1], 0))
    layer_out = split(widths(4)[7])
    three = reduce(me, *gradient(3))
    widths(3, *three.out)
    three.plane(before[0])
    two = reduce(me, *gradient(2, *three.out))
    widths(2, *two.out)
    three.along(before[0])
    two.plane(*three.out)
    send, keep = gradient(1, *two.out)
    two.along(keep, *three.arrived)
    one = reduce(me, send, keep, *two.out)
    one.plane(*two.out)
    input_grad, send, keep = attention_backward(
        tie(place, *one.out), inputs_rows, q, k, v, o, p,
        [split(states[quarter][4]) for quarter in (4, 3, 2, 1)],
        split(before[0]), weights.reshape(3, D, D), wo.reshape(D, D), before[1],
    )
    one.along(keep)
    attention = reduce(me, send, keep, *one.out, *two.arrived)
    attention.plane(*one.out)
    send, keep = gradient(0, *attention.out)
    attention.along(keep, *one.arrived)
    zero = reduce(me, send, keep, *attention.out)
    zero.plane(*attention.out)
    three_sum, two_sum, one_sum = [value.result(*zero.out) for value in (three, two, one)]
    attention_sum = attention.result(*zero.out)
    zero.along(*zero.out)
    sums = [zero.result(), one_sum, two_sum, three_sum]

    attention_gradient = jnp.stack(
        [attention_sum[index // 2][:, D * (index % 2) : D * (index % 2 + 1)] for index in range(4)]
    )
    feedforward_gradient = jnp.stack([jnp.concatenate([value[c] for value in sums], axis=1) for c in (0, 1)])
    if paired:
        table = attention.unit[0, :names, 2 * D : 2 * D + UNIT]
        vector_gradient = lax.dynamic_slice_in_dim(table, OWN * core, OWN, 1)
    else:
        table = in_rows(attention.keep)[:, 2 * D : 2 * D + UNIT].reshape(UNITS, UNIT, UNIT)[:, :names]
        table = table.transpose(1, 0, 2).reshape(names, D)
        vector_gradient = lax.psum_scatter(table, AXES, scatter_dimension=1, tiled=True)

    rate = 0.05 / math.sqrt(micro * length * count)
    return (
        layer_out[:, None],
        input_grad[:, None],
        *update(attention_weights, attention_momentum, attention_average, attention_gradient, rate),
        *update(feedforward_weights, feedforward_momentum, feedforward_average, feedforward_gradient, rate),
        *update(vector_weights, vector_momentum, vector_average, vector_gradient, rate),
    )


def solution(mesh):
    row = P(None, AXES, None, None)
    matrix = P(None, AXES, None)
    table = P(None, AXES)
    in_specs = (row, row, matrix) + (matrix,) * 6 + (table,) * 3
    out_specs = (row, row) + (matrix,) * 8 + (table,) * 4
    return jax.shard_map(body, mesh=mesh, in_specs=in_specs, out_specs=out_specs, check_vma=False)
```
